256 devices in a mesh: chan: 32 (over y, z_lo, x), tm: 8 (over z_hi, core).
Axes of the slice: x: 4, y: 4, z: 8 (z_hi: 4, z_lo: 2; z = z_hi * 2 + z_lo), core: 2. Of those that a mesh axis runs over, the one named last changes fastest.
Arguments:
- record: bfloat16 [8, 1024, 7680], P('tm', None, 'chan'), may hold values from -6 to 6
- fir_taps: bfloat16 [257], replicated, may hold values from -0.375 to 0.375
- sources: int32 [64], replicated, may hold values from 0 to 1023, as said below
- valid_mask: int32 [8, 1024], replicated, may hold values 0 or 1
Outputs:
- stack: float32 [64, 1024, 512], P('tm', 'chan')
The draws below stay inside these ranges and needn't reach their ends.
Inputs may be any that keep to these rules, and one draw needn't show every extreme that they name: `sources`: source s is one of the channels s * 16 to (s + 1) * 16 - 1; source 0 is channel 0 and the last source is the last channel.
All inputs are finite; a program needn't handle non-finite values.
Results may differ from the reference program's by a relative error of at most 0.011.
Values may be sent and summed in bfloat16 or wider, within the bound.
No kernel may reach another device: no remote copies, remote signals or barrier semaphores. Data moves between devices by JAX's collectives and lax.ppermute only.
A program may use at most 64 MiB of HBM per device.

```python
import math
import jax
import jax.numpy as jnp
from jax import lax

SAMPLES = 7680
TAPS = 257
FACTOR_A = 64
FACTOR_B = 128
MAXLAG = 256
LAGS = 512
VSOURCES = 64
CHANNELS = 1024
WINDOWS = 8
SPACING = 16


def draw_sources(key, part):
    key = jax.random.fold_in(key, 11)
    offsets = jax.random.randint(key, (VSOURCES,), 0, SPACING, dtype=jnp.int32)
    positions = jnp.arange(VSOURCES, dtype=jnp.int32)
    offsets = jnp.where(positions == 0, 0, offsets)
    offsets = jnp.where(positions == VSOURCES - 1, SPACING - 1, offsets)
    return positions * SPACING + offsets


def set_ends(array, key, smallest, top_value):
    spot = [jax.random.randint(jax.random.fold_in(key, axis), (), 0, length) for axis, length in enumerate(array.shape)]
    widest = array.shape.index(max(array.shape))
    beside = spot[:widest] + [(spot[widest] + 1) % array.shape[widest]] + spot[widest + 1:]
    return array.at[tuple(spot)].set(smallest).at[tuple(beside)].set(top_value)


def steps_of(stream_key, shape, pieces, low, largest):
    def one(axis_at, blocks):
        heights = jax.random.uniform(jax.random.fold_in(jax.random.fold_in(stream_key, 6), axis_at), (blocks,), jnp.float32, low / len(pieces), largest / len(pieces))
        return jnp.repeat(jnp.exp(heights), shape[axis_at] // blocks).reshape((-1,) + (1,) * (len(shape) - axis_at - 1))

    factor_of = one(*pieces[0])
    for cut in pieces[1:]:
        factor_of = factor_of * one(*cut)
    return factor_of


def centred(stream_key, dims, spread, limit, shards=(), kind=jnp.bfloat16):
    entries = jax.random.normal(stream_key, dims, jnp.float32) * spread
    if len(shards) > 0:
        entries = steps_of(stream_key, dims, shards, -0.22, 0.18) * entries
    return jnp.clip(entries, min=-limit, max=limit).astype(kind)


def setup_inputs(seed: int = 0) -> dict:
    keys = jax.random.split(jax.random.key(seed), 5)
    record = centred(keys[0], (WINDOWS, CHANNELS, SAMPLES), 1.0, 6.0, ((0, 8), (2, 32)))
    fir_taps = centred(keys[1], (TAPS,), TAPS ** -0.5, 0.375)
    sources = draw_sources(jax.random.fold_in(keys[4], 71), 0)
    valid_mask = set_ends((jax.random.randint(keys[3], (WINDOWS, CHANNELS), 0, 5) < 3).astype(jnp.int32), jax.random.fold_in(keys[3], 1), 0, 1)
    return dict(record=record, fir_taps=fir_taps, sources=sources, valid_mask=valid_mask)


def phase_table(left, right, period):
    product = left[:, None] * right[None, :] % period
    angles = product.astype(jnp.float32) * jnp.float32(2.0 * math.pi / period)
    return (jnp.cos(angles), jnp.sin(angles))

def rounded(values):
    return lax.optimization_barrier(values.astype(jnp.bfloat16)).astype(jnp.float32)

def mix(table, values, form):
    return jnp.einsum(form, table, values, precision=lax.Precision.HIGHEST)

def fir_rows(signal_rows, fir_taps):
    half_taps = (TAPS - 1) // 2
    signal = signal_rows.astype(jnp.float32)[:, None, :]
    kernel = fir_taps[::-1].astype(jnp.float32)[None, None, :]
    result = lax.conv_general_dilated(signal, kernel, (1,), [(half_taps, half_taps)], precision=lax.Precision.HIGHEST)
    return result[:, 0, :].astype(jnp.bfloat16)

def whiten(filtered):
    row_total = filtered.shape[0]
    span = FACTOR_A * FACTOR_B
    padded = jnp.pad(filtered, ((0, 0), (0, span - SAMPLES)))
    columns = padded.reshape(row_total, FACTOR_B, FACTOR_A).astype(jnp.float32)
    index_a = jnp.arange(FACTOR_A, dtype=jnp.int32)
    index_b = jnp.arange(FACTOR_B, dtype=jnp.int32)
    cos_b, sin_b = phase_table(index_b, index_b, FACTOR_B)
    zeta_re = jnp.einsum('rba,bk->rak', columns, rounded(cos_b), precision=lax.Precision.HIGHEST)
    zeta_im = -jnp.einsum('rba,bk->rak', columns, rounded(sin_b), precision=lax.Precision.HIGHEST)
    twist_cos, twist_sin = phase_table(index_a, index_b, span)
    twisted_re = rounded(zeta_re * twist_cos + zeta_im * twist_sin)
    twisted_im = rounded(zeta_im * twist_cos - zeta_re * twist_sin)
    cos_a, sin_a = phase_table(index_a, index_a, FACTOR_A)
    cos_a = rounded(cos_a)
    sin_a = rounded(sin_a)
    spec_re = mix(cos_a, twisted_re, 'ja,rak->rjk') + mix(sin_a, twisted_im, 'ja,rak->rjk')
    spec_im = mix(cos_a, twisted_im, 'ja,rak->rjk') - mix(sin_a, twisted_re, 'ja,rak->rjk')
    levels = lax.optimization_barrier(jnp.mean(jnp.sqrt(spec_re * spec_re + spec_im * spec_im), axis=-1, keepdims=True)) + 1e-05
    return ((spec_re / levels).astype(jnp.bfloat16), (spec_im / levels).astype(jnp.bfloat16))

def correlate(src_re, src_im, chan_re, chan_im):
    span = FACTOR_A * FACTOR_B
    source_re = src_re.astype(jnp.float32)[:, None]
    source_im = src_im.astype(jnp.float32)[:, None]
    channel_re = chan_re.astype(jnp.float32)[None]
    channel_im = chan_im.astype(jnp.float32)[None]
    cross_re = rounded(source_re * channel_re + source_im * channel_im)
    cross_im = rounded(source_im * channel_re - source_re * channel_im)
    index_a = jnp.arange(FACTOR_A, dtype=jnp.int32)
    index_b = jnp.arange(FACTOR_B, dtype=jnp.int32)
    cos_a, sin_a = phase_table(index_a, index_a, FACTOR_A)
    cos_a = rounded(cos_a)
    sin_a = rounded(sin_a)
    fold_re = mix(cos_a, cross_re, 'jk,sckb->scjb') - mix(sin_a, cross_im, 'jk,sckb->scjb')
    fold_im = mix(cos_a, cross_im, 'jk,sckb->scjb') + mix(sin_a, cross_re, 'jk,sckb->scjb')
    twist_cos, twist_sin = phase_table(index_a, index_b, span)
    turned_re = rounded(fold_re * twist_cos - fold_im * twist_sin)
    turned_im = rounded(fold_re * twist_sin + fold_im * twist_cos)
    lag_rows = jnp.concatenate([jnp.arange(FACTOR_B - MAXLAG // FACTOR_A, FACTOR_B, dtype=jnp.int32), jnp.arange(0, MAXLAG // FACTOR_A, dtype=jnp.int32)])
    cos_d, sin_d = phase_table(index_b, lag_rows, FACTOR_B)
    lagged = jnp.einsum('scjb,bd->scdj', turned_re, rounded(cos_d), precision=lax.Precision.HIGHEST)
    lagged = lagged - jnp.einsum('scjb,bd->scdj', turned_im, rounded(sin_d), precision=lax.Precision.HIGHEST)
    return lagged.reshape(lagged.shape[0], lagged.shape[1], LAGS) * jnp.float32(1.0 / math.sqrt(span))

def reference(record, fir_taps, sources, valid_mask):

    def window_white(window_rows):
        return whiten(fir_rows(window_rows, fir_taps))
    white_re, white_im = lax.map(window_white, record)
    src_re = jnp.take(white_re, sources, axis=1)
    src_im = jnp.take(white_im, sources, axis=1)
    valid_float = valid_mask.astype(jnp.float32)
    src_valid = jnp.take(valid_float, sources, axis=1)
    pair_count = jnp.dot(jnp.take(valid_mask, sources, axis=1).T, valid_mask)
    block_size = math.gcd(VSOURCES, 2)

    def per_block(block_index):
        first_row = block_index * block_size

        def per_window(running, window):
            part_re = lax.dynamic_slice_in_dim(src_re[window], first_row, block_size, 0)
            part_im = lax.dynamic_slice_in_dim(src_im[window], first_row, block_size, 0)
            weight = lax.dynamic_slice_in_dim(src_valid[window], first_row, block_size, 0)[:, None, None] * valid_float[window][None, :, None]
            return (running + weight * correlate(part_re, part_im, white_re[window], white_im[window]), None)
        running, _ = lax.scan(per_window, jnp.zeros((block_size, CHANNELS, LAGS), jnp.float32), jnp.arange(WINDOWS, dtype=jnp.int32))
        return running
    stack_sum = lax.map(per_block, jnp.arange(VSOURCES // block_size, dtype=jnp.int32)).reshape(VSOURCES, CHANNELS, LAGS)
    return stack_sum / jnp.maximum(pair_count, 1).astype(jnp.float32)[:, :, None]
```

```python
import functools
import math

import jax
import jax.numpy as jnp
import numpy as np
from jax import lax
from jax.experimental import pallas as pl
from jax.experimental.pallas import tpu as pltpu
from jax.sharding import PartitionSpec as P

SPAN = 8192
ROWS_B = 32
COLS_A = 256
HALF = 128
BAND = 128
MAXLAG = 256
LAGS = 512
TILE = 256
STEP_K2 = 4
ROW_STEP = 16
PLANES = ROWS_B + 1
BLOCK_ORDER = (2, 1, 3, 0)


def angle_tables(left, right, period):
    angles = (np.outer(left, right) % period) * (2.0 * math.pi / period)
    return np.cos(angles), np.sin(angles)


@functools.cache
def tables():
    b = np.arange(ROWS_B)
    a = np.arange(COLS_A)
    k1 = np.arange(HALF)
    cos_b, sin_b = angle_tables(b, b, ROWS_B)
    first = np.concatenate([cos_b, -sin_b], axis=0)
    twist = np.stack(angle_tables(b, a, SPAN)).astype(np.float32)
    cos_a, sin_a = angle_tables(a, k1, COLS_A)
    second = np.concatenate(
        [np.concatenate([cos_a, -sin_a], axis=1), np.concatenate([sin_a, cos_a], axis=1)], axis=0
    )
    bins = b[:, None] + ROWS_B * k1[None, :]
    shift = np.stack([np.cos(bins * math.pi / SPAN), np.sin(bins * math.pi / SPAN)])
    odd = 2 * np.arange(MAXLAG) + 1
    angles = (np.outer(bins.reshape(-1), odd) % (2 * SPAN)) * (math.pi / SPAN)
    scale = 1.0 / math.sqrt(SPAN)
    lag_cos = (np.cos(angles) * scale).reshape(ROWS_B, HALF, MAXLAG)
    lag_sin = (np.sin(angles) * scale).reshape(ROWS_B, HALF, MAXLAG)
    lag_sin[0, 0] = scale * (1 - 2 * (np.arange(MAXLAG) % 2))
    band = k1 // 4
    same = (band[:, None] == band[None, :]).astype(np.float32)
    lead = (k1 % 4 == 0)[:, None]
    following = (k1[:, None] == 4 * (band[None, :] + 1)).astype(np.float32)
    mirror_rest, mirror_edge = same, same * ~lead + following
    back = np.where(k1 % 4 == 0, np.maximum(k1 - 1, 0), k1)
    sums = np.concatenate(
        [
            np.concatenate([same, mirror_rest, mirror_rest[:, back]], axis=1),
            np.concatenate([same, mirror_edge, mirror_edge[:, back]], axis=1),
        ],
        axis=0,
    )
    nyquist = np.zeros((1, 3 * HALF), np.float32)
    nyquist[0, HALF + 124 : 2 * HALF] = 1.0
    nyquist[0, 2 * HALF + 125 :] = 1.0
    signs = (1.0 - 2.0 * (np.arange(COLS_A) % 2))[None].astype(np.float32)
    bf16 = jnp.bfloat16
    return dict(
        signs=signs,
        turn=np.eye(MAXLAG)[::-1].astype(bf16),
        first=first.astype(bf16),
        twist=twist,
        second=second.astype(bf16),
        shift=shift.astype(np.float32),
        lag_cos=lag_cos.astype(bf16),
        lag_sin=lag_sin.astype(bf16),
        sums=sums.astype(np.float32),
        nyquist=nyquist,
    )


def toeplitz_kernel(taps_ref, out_ref):
    rows, width = out_ref.shape
    base = jnp.broadcast_to(taps_ref[...], (rows, taps_ref.shape[1]))
    turned = pltpu.roll(base, taps_ref.shape[1] - MAXLAG, 1, stride=1, stride_axis=0)
    out_ref[...] = turned[:, :width].astype(out_ref.dtype)


def toeplitz_of(fir_taps):
    length = 2 * TILE + TILE
    base = jnp.pad(fir_taps.astype(jnp.float32), (0, 1024 - fir_taps.shape[0]))[None, :]
    return pl.pallas_call(
        toeplitz_kernel, out_shape=jax.ShapeDtypeStruct((2 * TILE, TILE), jnp.bfloat16)
    )(base)


def front_kernel(rotate, signal_ref, toeplitz_ref, first_ref, twist_ref, second_ref, sums_ref, nyquist_ref,
                 signs_ref, shift_ref, mask_ref, out_ref, filtered, twisted, spectrum, edge):
    rows = signal_ref.shape[0]
    count = signal_ref.shape[1] // TILE - 1
    f32, bf16 = jnp.float32, jnp.bfloat16
    tiles = jnp.concatenate([signal_ref[:, n * TILE : n * TILE + 2 * TILE] for n in range(count)], axis=0)
    made = jnp.dot(tiles, toeplitz_ref[...], preferred_element_type=f32)
    made = made.astype(bf16).astype(f32)
    for h in range(2):
        filtered[h, : count * rows] = made[:, h * HALF : (h + 1) * HALF]
        filtered[h, count * rows :] = jnp.zeros(((ROWS_B - count) * rows, HALF), f32)
    cos, sin = twist_ref[0], twist_ref[1]
    for r in range(rows):
        columns = [filtered[h, pl.ds(r, ROWS_B, stride=rows), :].astype(bf16) for h in range(2)]
        columns = jnp.concatenate(columns, axis=1)
        zeta = jnp.dot(first_ref[...], columns, preferred_element_type=f32)
        zeta_re, zeta_im = zeta[:ROWS_B], zeta[ROWS_B:]
        twisted_re = (zeta_re * cos + zeta_im * sin).astype(bf16)
        twisted_im = (zeta_im * cos - zeta_re * sin).astype(bf16)
        twisted[r * ROWS_B : (r + 1) * ROWS_B, :COLS_A] = twisted_re
        twisted[r * ROWS_B : (r + 1) * ROWS_B, COLS_A:] = twisted_im
        edge[r : r + 1, :] = twisted_re.astype(f32)[0:1]
    made = jnp.dot(twisted[...], second_ref[...], preferred_element_type=f32)
    spectrum[0], spectrum[1] = made[:, :HALF], made[:, HALF:]
    nyquist = jnp.sum(edge[...] * signs_ref[...], axis=1, keepdims=True)

    def plane(k2):
        return tuple(spectrum[h, pl.ds(k2, rows, stride=ROWS_B), :] for h in range(2))

    def size(k2):
        re, im = plane(k2)
        return jnp.sqrt(re * re + im * im)

    rest = size(1)
    for k2 in range(2, ROWS_B):
        rest = rest + size(k2)
    both = jnp.concatenate([rest, size(0)], axis=1)
    sums = jnp.dot(both, sums_ref[...], precision=lax.Precision.HIGHEST, preferred_element_type=f32)
    sums = sums + jnp.abs(nyquist) * nyquist_ref[...]
    levels = sums * (1.0 / BAND) + 1e-05
    level, mirror, mirror_lead = levels[:, :HALF], levels[:, HALF : 2 * HALF], levels[:, 2 * HALF :]
    lane = lax.broadcasted_iota(jnp.int32, (rows, HALF), 1)
    mask = mask_ref[...]
    gain = mask / level
    white_nyquist = mask * nyquist / mirror[:, HALF - 1 :]
    for k2 in range(ROWS_B):
        re, im = plane(k2)
        re, im = re * gain, im * gain
        if rotate:
            turn_cos, turn_sin = shift_ref[0, k2 : k2 + 1, :], shift_ref[1, k2 : k2 + 1, :]
            re, im = re * turn_cos + im * turn_sin, im * turn_cos - re * turn_sin
        if k2 == 0:
            im = jnp.where(lane == 0, white_nyquist, im)
        out_ref[k2, :, :HALF] = re.astype(bf16)
        out_ref[k2, :, HALF:] = im.astype(bf16)
    out_ref[ROWS_B, :, :HALF] = (level / mirror).astype(bf16)
    out_ref[ROWS_B, :, HALF:] = jnp.where(lane == 0, 0.0, level / mirror_lead).astype(bf16)


def front(signal, toeplitz, mask, first_row, rows, rotate):
    tab = tables()
    constants = [tab[k] for k in ("first", "twist", "second", "sums", "nyquist", "signs", "shift")]
    start = first_row // ROW_STEP

    def whole(array):
        return pl.BlockSpec(array.shape, lambda i, rank=array.ndim: (0,) * rank)

    length = signal.shape[1]
    return pl.pallas_call(
        functools.partial(front_kernel, rotate),
        grid=(rows // ROW_STEP,),
        in_specs=[pl.BlockSpec((ROW_STEP, length), lambda i: (start + i, 0)), whole(toeplitz)]
        + [whole(c) for c in constants]
        + [pl.BlockSpec((ROW_STEP, 1), lambda i: (i, 0))],
        out_specs=pl.BlockSpec((PLANES, ROW_STEP, 2 * HALF), lambda i: (0, i, 0)),
        out_shape=jax.ShapeDtypeStruct((PLANES, rows, 2 * HALF), jnp.bfloat16),
        scratch_shapes=[
            pltpu.VMEM((2, ROWS_B * ROW_STEP, HALF), jnp.float32),
            pltpu.VMEM((ROWS_B * ROW_STEP, 2 * COLS_A), jnp.bfloat16),
            pltpu.VMEM((2, ROWS_B * ROW_STEP, HALF), jnp.float32),
            pltpu.VMEM((ROW_STEP, COLS_A), jnp.float32),
        ],
        compiler_params=pltpu.CompilerParams(vmem_limit_bytes=40 * 1024 * 1024),
        cost_estimate=pl.CostEstimate(flops=rows * 20_000_000, bytes_accessed=rows * 40_000, transcendentals=0),
        name="front",
    )(signal, toeplitz, *constants, mask)


def correlate_kernel(src0, src1, sratio0, sratio1, chan0, chan1, cratio0, cratio1, cos_ref, sin_ref, turn_ref,
                     out0, out1, even, odd, weight, lead_weight, chan_wide, spread_out):
    step = pl.program_id(0)
    chans = chan0.shape[1]
    sources = src0.shape[1]
    f32, bf16 = jnp.float32, jnp.bfloat16
    srcs, chan_refs = (src0, src1), (chan0, chan1)

    def spread(row):
        return jnp.broadcast_to(row, (sources, HALF)).astype(bf16)

    @pl.when(step == 0)
    def _():
        for w, (sratio, cratio) in enumerate(((sratio0, cratio0), (sratio1, cratio1))):
            chan_wide[w, 0] = cratio[0].astype(f32)
            for c in range(chans):
                row = chan_wide[w, 0, pl.ds(c, 1), :]
                weight[w, c] = 1.0 + sratio[0, :, :HALF] * spread(row[:, :HALF])
                lead_weight[w, c] = 1.0 + sratio[0, :, HALF:] * spread(row[:, HALF:])

    for w in range(2):
        chan_wide[w] = chan_refs[w][...].astype(f32)

    def products(with_lead):
        parts_re, parts_im = [], []
        lane = lax.broadcasted_iota(jnp.int32, (sources, HALF), 1)
        keep = jnp.where(lane == 0, 0.0, 1.0).astype(bf16)
        only = jnp.where(lane == 0, 1.0, 0.0).astype(bf16)
        for c in range(chans):
            row_re, row_im = [], []
            for j in range(STEP_K2):
                total_re = total_im = None
                for w in range(2):
                    src_re, src_im = srcs[w][j, :, :HALF], srcs[w][j, :, HALF:]
                    chan_re = spread(chan_wide[w, j, pl.ds(c, 1), :HALF])
                    chan_im = spread(chan_wide[w, j, pl.ds(c, 1), HALF:])
                    same_re, same_im = src_re * chan_re, src_im * chan_im
                    mixed = src_im * chan_re - src_re * chan_im
                    if with_lead and j == 0:
                        scale = lead_weight[w, c]
                        part_re = (same_re + same_im * keep) * scale
                        part_im = (mixed * keep - same_im * only) * scale
                    else:
                        scale = weight[w, c]
                        part_re = (same_re + same_im) * scale
                        part_im = mixed * scale
                    total_re = part_re if w == 0 else total_re + part_re
                    total_im = part_im if w == 0 else total_im + part_im
                row_re.append(total_re)
                row_im.append(total_im)
            parts_re.append(jnp.concatenate(row_re, axis=1))
            parts_im.append(jnp.concatenate(row_im, axis=1))
        whole_re = jnp.concatenate(parts_re, axis=0)
        whole_im = jnp.concatenate(parts_im, axis=0)
        table_cos = cos_ref[...].reshape(STEP_K2 * HALF, MAXLAG)
        table_sin = sin_ref[...].reshape(STEP_K2 * HALF, MAXLAG)
        return (
            jnp.dot(whole_re, table_cos, preferred_element_type=f32),
            jnp.dot(whole_im, table_sin, preferred_element_type=f32),
        )

    @pl.when(step == 0)
    def _():
        even[...], odd[...] = products(True)

    @pl.when(step > 0)
    def _():
        part_even, part_odd = products(False)
        even[...] += part_even
        odd[...] += part_odd

    @pl.when(step == pl.num_programs(0) - 1)
    def _():
        early = (even[...] + odd[...]).astype(bf16)
        early = jnp.dot(early, turn_ref[...], preferred_element_type=f32)
        late = even[...] - odd[...]
        half = sources // 2
        for c in range(chans):
            for e in range(2):
                at = c * sources + e * half
                for q, (part, lanes) in enumerate(((early, 0), (early, HALF), (late, 0), (late, HALF))):
                    spread_out[e, q, pl.ds(c, half, stride=chans), :] = part[at : at + half, lanes : lanes + HALF]
        for q in range(LAGS // HALF):
            out0[:, q * HALF : (q + 1) * HALF] = spread_out[0, q].astype(out0.dtype)
            out1[:, q * HALF : (q + 1) * HALF] = spread_out[1, q].astype(out1.dtype)


def correlate(srcs, chans, half, types):
    tab = tables()
    sources = srcs[0].shape[1] // 2
    count = chans[0].shape[1]
    steps = ROWS_B // STEP_K2
    rows = count * sources
    src_spec = pl.BlockSpec((STEP_K2, sources, 2 * HALF), lambda i: (i, half, 0))
    src_ratio = pl.BlockSpec((1, sources, 2 * HALF), lambda i: (ROWS_B, half, 0))
    chan_spec = pl.BlockSpec((STEP_K2, count, 2 * HALF), lambda i: (i, 0, 0))
    chan_ratio = pl.BlockSpec((1, count, 2 * HALF), lambda i: (ROWS_B, 0, 0))
    table = pl.BlockSpec((STEP_K2, HALF, MAXLAG), lambda i: (i, 0, 0))
    out_spec = pl.BlockSpec((rows // 2, LAGS), lambda i: (0, 0))
    return pl.pallas_call(
        correlate_kernel,
        grid=(steps,),
        in_specs=[src_spec, src_spec, src_ratio, src_ratio, chan_spec, chan_spec, chan_ratio, chan_ratio]
        + [table, table, pl.BlockSpec((MAXLAG, MAXLAG), lambda i: (0, 0))],
        out_specs=[out_spec, out_spec],
        out_shape=[jax.ShapeDtypeStruct((rows // 2, LAGS), t) for t in types],
        scratch_shapes=[
            pltpu.VMEM((rows, MAXLAG), jnp.float32),
            pltpu.VMEM((rows, MAXLAG), jnp.float32),
            pltpu.VMEM((2, count, sources, HALF), jnp.bfloat16),
            pltpu.VMEM((2, count, sources, HALF), jnp.bfloat16),
            pltpu.VMEM((2, STEP_K2, count, 2 * HALF), jnp.float32),
            pltpu.VMEM((2, LAGS // HALF, rows // 2, HALF), jnp.float32),
        ],
        compiler_params=pltpu.CompilerParams(vmem_limit_bytes=40 * 1024 * 1024),
        cost_estimate=pl.CostEstimate(
            flops=4 * rows * SPAN * MAXLAG, bytes_accessed=8 * 1024 * 1024, transcendentals=0
        ),
        name="correlate",
    )(srcs[0], srcs[1], srcs[0], srcs[1], chans[0], chans[1], chans[0], chans[1],
      tab["lag_cos"], tab["lag_sin"], tab["turn"])


def source_order(time_index):
    row = jnp.arange(64, dtype=jnp.int32)
    relative = jnp.asarray(BLOCK_ORDER, jnp.int32)[(row // 8) % 4]
    z_hi = (time_index // 2 + relative) % 4
    parity = (time_index % 2 + row // 32) % 2
    return (2 * z_hi + parity) * 8 + row % 8


def body(record, fir_taps, sources, valid_mask):
    chan_count = lax.axis_size("chan")
    time_count = lax.axis_size("tm")
    _, channels, part_len = record.shape
    chan_local = channels // chan_count
    source_total = sources.shape[0]
    chan_index = lax.axis_index("chan")
    time_index = lax.axis_index("tm")
    first_chan = chan_index * chan_local

    ordered = jnp.take(sources, source_order(time_index))
    every_channel = jnp.arange(channels, dtype=jnp.int32)
    picker = (ordered[:, None] == every_channel[None, :]).astype(jnp.bfloat16)
    source_rows = jnp.dot(picker, record[0], preferred_element_type=jnp.float32).astype(jnp.bfloat16)
    grouped = record.reshape(chan_count, chan_local, part_len)
    sent = jnp.concatenate(
        [jnp.broadcast_to(source_rows[None], (chan_count,) + source_rows.shape), grouped], axis=1
    )
    pieces = lax.all_to_all(sent, "chan", split_axis=0, concat_axis=0, tiled=True)
    signal = pieces.transpose(1, 0, 2).reshape(source_total + chan_local, chan_count * part_len)
    signal = jnp.pad(signal, ((0, 0), (HALF, HALF)))

    toeplitz = toeplitz_of(fir_taps)
    valid_float = valid_mask.astype(jnp.float32)
    window_valid = lax.dynamic_index_in_dim(valid_float, time_index, 0, keepdims=False)
    source_mask = jnp.sum(jnp.where(picker > 0, window_valid[None, :], 0.0), axis=1, keepdims=True)
    chan_valid = lax.dynamic_slice_in_dim(valid_float, first_chan, chan_local, 1)
    chan_mask = lax.dynamic_slice_in_dim(window_valid, first_chan, chan_local, 0)[:, None]
    rows_out = source_total // time_count
    own_sources = lax.dynamic_slice_in_dim(sources, time_index * rows_out, rows_out, 0)
    own_picker = (own_sources[:, None] == every_channel[None, :]).astype(jnp.float32)
    own_valid = jnp.dot(own_picker, valid_float.T, precision=lax.Precision.HIGHEST)
    pair_count = jnp.dot(own_valid, chan_valid, precision=lax.Precision.HIGHEST)

    swap = [(j, j ^ 1) for j in range(time_count)]
    per_core = source_total // 2
    away = front(signal, toeplitz, source_mask[per_core:], per_core, per_core, True)
    away = lax.ppermute(away, "tm", swap)
    chan = front(signal, toeplitz, chan_mask, source_total, chan_local, False)
    other_chan = lax.ppermute(chan, "tm", swap)
    near = front(signal, toeplitz, source_mask[:per_core], 0, per_core, True)

    def along(block, values):
        return lax.ppermute(values, "tm", [(j, (j + 2 * block) % time_count) for j in range(time_count)])

    bf16 = jnp.bfloat16
    first = correlate((near, away), (chan, other_chan), 0, (bf16, bf16))
    total = along(BLOCK_ORDER[0], first[0]).astype(jnp.float32) + along(BLOCK_ORDER[1], first[1])
    second = correlate((near, away), (chan, other_chan), 1, (bf16, jnp.float32))
    total = total + along(BLOCK_ORDER[2], second[0]) + second[1]
    stack = total.reshape(rows_out, chan_local, LAGS)
    return stack / jnp.maximum(pair_count, 1.0)[:, :, None]


def solution(mesh):
    return jax.shard_map(
        body,
        mesh=mesh,
        in_specs=(P("tm", None, "chan"), P(), P(), P()),
        out_specs=P("tm", "chan", None),
        check_vma=False,
    )
```

```python
import functools
import math

import jax
import jax.numpy as jnp
import numpy as np
from jax import lax
from jax.experimental import pallas as pl
from jax.experimental.pallas import tpu as pltpu
from jax.sharding import PartitionSpec as P

SPAN = 8192
SAMPLES = 7680
ROWS_B = 32
COLS_A = 256
HALF = 128
BAND = 128
MAXLAG = 256
LAGS = 512
TILE = 256
STEP_K2 = 16
ROW_STEP = 16
ROW_PART = 8
VMEM_LIMIT = 16 * 1024 * 1024
PLANES = ROWS_B + 1


def angle_tables(left, right, period):
    angles = (np.outer(left, right) % period) * (2.0 * math.pi / period)
    return np.cos(angles), np.sin(angles)


@functools.cache
def tables():
    b = np.arange(ROWS_B)
    a = np.arange(COLS_A)
    k1 = np.arange(HALF)
    cos_b, sin_b = angle_tables(b, b, ROWS_B)
    used = np.concatenate([cos_b, -sin_b], axis=0)[:, : SAMPLES // COLS_A]
    first = np.kron(used, np.eye(ROW_PART))
    twist = np.stack(angle_tables(b, a, SPAN)).astype(np.float32)
    cos_a, sin_a = angle_tables(a, k1, COLS_A)
    second = np.concatenate(
        [np.concatenate([cos_a, -sin_a], axis=1), np.concatenate([sin_a, cos_a], axis=1)], axis=0
    )
    bins = b[:, None] + ROWS_B * k1[None, :]
    shift = np.stack([np.cos(bins * math.pi / SPAN), np.sin(bins * math.pi / SPAN)])
    odd = 2 * np.arange(MAXLAG) + 1
    angles = (np.outer(bins.reshape(-1), odd) % (2 * SPAN)) * (math.pi / SPAN)
    scale = 1.0 / math.sqrt(SPAN)
    lag_cos = (np.cos(angles) * scale).reshape(ROWS_B, HALF, MAXLAG)
    lag_sin = (np.sin(angles) * scale).reshape(ROWS_B, HALF, MAXLAG)
    lag_sin[0, 0] = scale * (1 - 2 * (np.arange(MAXLAG) % 2))
    band = k1 // 4
    same = (band[:, None] == band[None, :]).astype(np.float32)
    lead = (k1 % 4 == 0)[:, None]
    following = (k1[:, None] == 4 * (band[None, :] + 1)).astype(np.float32)
    mirror_rest, mirror_edge = same, same * ~lead + following
    back = np.where(k1 % 4 == 0, np.maximum(k1 - 1, 0), k1)
    sums = np.concatenate(
        [
            np.concatenate([same, mirror_rest, mirror_rest[:, back]], axis=1),
            np.concatenate([same, mirror_edge, mirror_edge[:, back]], axis=1),
        ],
        axis=0,
    )
    nyquist = np.zeros((1, 3 * HALF), np.float32)
    nyquist[0, HALF + 124 : 2 * HALF] = 1.0
    nyquist[0, 2 * HALF + 125 :] = 1.0
    signs = (1.0 - 2.0 * (np.arange(COLS_A) % 2))[None].astype(np.float32)
    bf16 = jnp.bfloat16
    return dict(
        turn=np.eye(MAXLAG)[::-1].astype(bf16),
        products=np.concatenate(
            [np.pad(first, ((0, 0), (0, COLS_A - first.shape[1]))), second, sums[:, : 2 * HALF]]
            + [np.pad(sums[:, 2 * HALF :], ((0, 0), (0, HALF)))]
        ).astype(bf16),
        rotations=np.concatenate(
            [twist[0], twist[1], np.concatenate([shift[0], shift[1]], axis=1)]
            + [np.repeat(v, 8, axis=0) for v in (signs, nyquist[:, : 2 * HALF])]
            + [np.repeat(np.pad(nyquist[:, 2 * HALF :], ((0, 0), (0, HALF))), 8, axis=0)]
        ).astype(np.float32),
        lags=np.stack([lag_cos, lag_sin], axis=1).astype(bf16),
    )


def toeplitz_kernel(taps_ref, out_ref):
    rows, width = out_ref.shape
    base = jnp.broadcast_to(taps_ref[...], (rows, taps_ref.shape[1]))
    turned = pltpu.roll(base, taps_ref.shape[1] - MAXLAG, 1, stride=1, stride_axis=0)
    out_ref[...] = turned[:, :width].astype(out_ref.dtype)


def toeplitz_of(fir_taps):
    length = 2 * TILE + TILE
    base = jnp.pad(fir_taps.astype(jnp.float32), (0, 1024 - fir_taps.shape[0]))[None, :]
    return pl.pallas_call(
        toeplitz_kernel,
        out_shape=jax.ShapeDtypeStruct((2 * TILE, TILE), jnp.bfloat16),
        compiler_params=pltpu.CompilerParams(vmem_limit_bytes=VMEM_LIMIT),
    )(base)


def gather_kernel(sources_ref, record_ref, out_ref, picked):
    sources = sources_ref.shape[1]
    count, rows, _ = out_ref.shape
    own = rows - sources
    step = pl.program_id(0)
    turned = (((1,), (1,)), ((), ()))

    def pick(rows_wanted, values):
        channel = lax.broadcasted_iota(jnp.int32, (rows_wanted.shape[0], values.shape[1]), 1)
        picker = jnp.where(channel == rows_wanted, 1.0, 0.0).astype(jnp.bfloat16)
        rows_of = lax.dot_general(picker, values, turned, preferred_element_type=jnp.float32)
        return rows_of.astype(jnp.bfloat16)

    @pl.when(step == 0)
    def _():
        order = source_order(lax.axis_index("tm"), (sources, sources))
        lane = lax.broadcasted_iota(jnp.int32, (sources, sources), 1)
        channels = jnp.where(lane == order, sources_ref[...].astype(jnp.float32), 0.0)
        channels = jnp.sum(channels, axis=1, keepdims=True).astype(jnp.int32)
        picked[...] = pick(channels, record_ref[...])

    here = pl.ds(pl.multiple_of(step * (count * own), count * own), count * own)
    straight = lax.broadcasted_iota(jnp.int32, (count * own, 1), 0)
    mine = pick(straight, record_ref[:, here])
    for i in range(count):
        out_ref[i, :sources] = picked[...]
        out_ref[i, sources:] = mine[i * own : (i + 1) * own]


def in_hbm(array):
    return pltpu.with_memory_space_constraint(array, pltpu.HBM)


def gather_rows(sources, record, chan_count):
    length, channels = record.shape
    total = sources.shape[0]
    rows = total + channels // chan_count
    steps = 4
    return pl.pallas_call(
        gather_kernel,
        grid=(steps,),
        in_specs=[
            pl.BlockSpec((1, total), lambda i: (0, 0)),
            pl.BlockSpec((length, channels), lambda i: (0, 0)),
        ],
        out_specs=pl.BlockSpec((chan_count // steps, rows, length), lambda i: (i, 0, 0)),
        out_shape=jax.ShapeDtypeStruct((chan_count, rows, length), jnp.bfloat16),
        scratch_shapes=[pltpu.VMEM((total, length), jnp.bfloat16)],
        compiler_params=pltpu.CompilerParams(vmem_limit_bytes=VMEM_LIMIT),
        name="gather",
    )(in_hbm(sources[None, :]), in_hbm(record))


def front_kernel(rotated, pieces_ref, toeplitz_ref, products_ref, rotations_ref, mask_ref, out_ref, signal):
    count, rows, part = pieces_ref.shape
    length = count * part
    f32, bf16 = jnp.float32, jnp.bfloat16
    signal[:, :HALF] = jnp.zeros((rows, HALF), bf16)
    signal[:, HALF + length :] = jnp.zeros((rows, HALF), bf16)
    for i in range(count):
        signal[:, HALF + i * part : HALF + (i + 1) * part] = pieces_ref[i]
    tiles = jnp.concatenate(
        [signal[:, n * TILE : n * TILE + 2 * TILE] for n in range(length // TILE)], axis=0
    )
    made = jnp.dot(tiles, toeplitz_ref[...], preferred_element_type=f32)
    made = made.reshape(length // TILE, rows, TILE)
    zetas = []
    split = 2 * ROWS_B * ROW_PART
    for part in range(rows // ROW_PART):
        filtered = made[:, part * ROW_PART : (part + 1) * ROW_PART].reshape(-1, TILE).astype(bf16)
        zetas.append(jnp.dot(products_ref[:split, : filtered.shape[0]], filtered, preferred_element_type=f32))
    turned_re, turned_im = [], []
    for k2 in range(ROWS_B):
        cos = jnp.broadcast_to(rotations_ref[k2 : k2 + 1, :], (ROW_PART, COLS_A))
        sin = jnp.broadcast_to(rotations_ref[ROWS_B + k2 : ROWS_B + k2 + 1, :], (ROW_PART, COLS_A))
        for zeta in zetas:
            zeta_re = zeta[k2 * ROW_PART : (k2 + 1) * ROW_PART]
            zeta_im = zeta[(ROWS_B + k2) * ROW_PART : (ROWS_B + k2 + 1) * ROW_PART]
            turned_re.append(zeta_re * cos + zeta_im * sin)
            turned_im.append(zeta_im * cos - zeta_re * sin)
    twisted_re = jnp.concatenate(turned_re, axis=0).astype(bf16)
    twisted_im = jnp.concatenate(turned_im, axis=0).astype(bf16)
    nyquist = jnp.sum(twisted_re[:rows].astype(f32) * rotations_ref[3 * ROWS_B : 3 * ROWS_B + 1], axis=1, keepdims=True)
    twisted = jnp.concatenate([twisted_re, twisted_im], axis=1)
    spectrum = jnp.dot(twisted, products_ref[split : split + 2 * COLS_A], preferred_element_type=f32)
    re, im = spectrum[:, :HALF], spectrum[:, HALF:]

    size = jnp.sqrt(re * re + im * im)
    rest = jnp.sum(size[rows:].reshape(ROWS_B - 1, rows, HALF), axis=0)
    both = jnp.concatenate([rest, size[:rows]], axis=1)
    high = both.astype(bf16)
    left = both - high.astype(f32)
    middle = left.astype(bf16)
    low = (left - middle.astype(f32)).astype(bf16)
    split += 2 * COLS_A
    parts = jnp.concatenate([high, middle, low], axis=0)
    parts = [
        jnp.dot(parts, products_ref[at : at + 2 * HALF], preferred_element_type=f32)
        for at in (split, split + 2 * HALF)
    ]
    parts = jnp.concatenate([parts[0], parts[1][:, :HALF]], axis=1)
    sums = parts[:rows] + parts[rows : 2 * rows] + parts[2 * rows :]
    at = 3 * ROWS_B + 8
    first_part, last_part = rotations_ref[at : at + 1], rotations_ref[at + 8 : at + 9, :HALF]
    sums = sums + jnp.abs(nyquist) * jnp.concatenate([first_part, last_part], axis=1)
    levels = sums * (1.0 / BAND) + 1e-05
    level, mirror, mirror_lead = levels[:, :HALF], levels[:, HALF : 2 * HALF], levels[:, 2 * HALF :]
    lane = lax.broadcasted_iota(jnp.int32, (rows, HALF), 1)
    mask = mask_ref[...]
    gain = mask / level
    white_nyquist = mask[:, :1] * nyquist / mirror[:, HALF - 1 :]
    ratio = (level / mirror).astype(bf16)
    ratio_lead = jnp.where(lane == 0, 0.0, level / mirror_lead).astype(bf16)

    def write(out_ref, rotate):
        for k2 in range(ROWS_B):
            here = slice(k2 * rows, (k2 + 1) * rows)
            white_re, white_im = re[here] * gain, im[here] * gain
            if rotate:
                turns = rotations_ref[2 * ROWS_B + k2 : 2 * ROWS_B + k2 + 1, :]
                turn_cos = jnp.broadcast_to(turns[:, :HALF], (rows, HALF))
                turn_sin = jnp.broadcast_to(turns[:, HALF:], (rows, HALF))
                white_re, white_im = (
                    white_re * turn_cos + white_im * turn_sin,
                    white_im * turn_cos - white_re * turn_sin,
                )
            if k2 == 0:
                white_im = jnp.where(lane == 0, white_nyquist, white_im)
            out_ref[k2, :, :HALF] = white_re.astype(bf16)
            out_ref[k2, :, HALF:] = white_im.astype(bf16)
        out_ref[ROWS_B, :, :HALF] = ratio
        out_ref[ROWS_B, :, HALF:] = ratio_lead

    is_source = pl.program_id(0) < rotated
    pl.when(is_source)(lambda: write(out_ref, True))
    pl.when(jnp.logical_not(is_source))(lambda: write(out_ref, False))


def front(pieces, toeplitz, mask, start, rows, rotated):
    tab = tables()
    count, _, part = pieces.shape
    start = start // ROW_STEP

    def whole(array):
        return pl.BlockSpec(array.shape, lambda i, rank=array.ndim: (0,) * rank)

    return pl.pallas_call(
        functools.partial(front_kernel, rotated // ROW_STEP),
        grid=(rows // ROW_STEP,),
        in_specs=[
            pl.BlockSpec((count, ROW_STEP, part), lambda i: (0, start + i, 0)),
            whole(toeplitz),
            whole(tab["products"]),
            whole(tab["rotations"]),
            pl.BlockSpec((ROW_STEP, HALF), lambda i: (start + i, 0)),
        ],
        out_specs=pl.BlockSpec((PLANES, ROW_STEP, 2 * HALF), lambda i: (0, i, 0)),
        out_shape=jax.ShapeDtypeStruct((PLANES, rows, 2 * HALF), jnp.bfloat16),
        scratch_shapes=[pltpu.VMEM((ROW_STEP, count * part + 2 * HALF), jnp.bfloat16)],
        compiler_params=pltpu.CompilerParams(vmem_limit_bytes=VMEM_LIMIT),
        cost_estimate=pl.CostEstimate(flops=rows * 20_000_000, bytes_accessed=4_000_000, transcendentals=0),
        name="front",
    )(in_hbm(pieces), toeplitz, in_hbm(jnp.asarray(tab["products"])), tab["rotations"], mask)


def correlate_kernel(src0, src1, sratio0, sratio1, chan0, chan1, cratio0, cratio1, lags_ref, turn_ref,
                     *rest):
    outs, (even, odd, weight, lead_weight, src_wide) = rest[:-5], rest[-5:]
    step = pl.program_id(0)
    chans = chan0.shape[1]
    sources = src0.shape[1]
    f32, bf16 = jnp.float32, jnp.bfloat16
    srcs, chan_refs = (src0, src1), (chan0, chan1)

    def spread(w, j, s, h):
        return jnp.broadcast_to(src_wide[w, j, h, pl.ds(s, 1), :], (chans, HALF)).astype(bf16)

    @pl.when(step == 0)
    def _():
        for w, (sratio, cratio) in enumerate(((sratio0, cratio0), (sratio1, cratio1))):
            for h in range(2):
                src_wide[w, 0, h] = sratio[0, :, h * HALF : (h + 1) * HALF].astype(f32)
            for s in range(sources):
                weight[w, s] = 1.0 + cratio[0, :, :HALF] * spread(w, 0, s, 0)
                lead_weight[w, s] = 1.0 + cratio[0, :, HALF:] * spread(w, 0, s, 1)

    for w in range(2):
        for h in range(2):
            src_wide[w, :, h] = srcs[w][:, :, h * HALF : (h + 1) * HALF].astype(f32)

    def products(with_lead):
        parts_re, parts_im = [], []
        lane = lax.broadcasted_iota(jnp.int32, (chans, HALF), 1)
        keep = jnp.where(lane == 0, 0.0, 1.0).astype(bf16)
        only = jnp.where(lane == 0, 1.0, 0.0).astype(bf16)
        for s in range(sources):
            row_re, row_im = [], []
            for j in range(STEP_K2):
                total_re = total_im = None
                for w in range(2):
                    chan_re, chan_im = chan_refs[w][j, :, :HALF], chan_refs[w][j, :, HALF:]
                    src_re, src_im = spread(w, j, s, 0), spread(w, j, s, 1)
                    same_re, same_im = src_re * chan_re, src_im * chan_im
                    mixed = src_im * chan_re - src_re * chan_im
                    if with_lead and j == 0:
                        scale = lead_weight[w, s]
                        part_re = (same_re + same_im * keep) * scale
                        part_im = (mixed * keep - same_im * only) * scale
                    else:
                        scale = weight[w, s]
                        part_re = (same_re + same_im) * scale
                        part_im = mixed * scale
                    total_re = part_re if w == 0 else total_re + part_re
                    total_im = part_im if w == 0 else total_im + part_im
                row_re.append(total_re)
                row_im.append(total_im)
            parts_re.append(jnp.concatenate(row_re, axis=1))
            parts_im.append(jnp.concatenate(row_im, axis=1))
        table_cos = lags_ref[:, 0].reshape(STEP_K2 * HALF, MAXLAG)
        table_sin = lags_ref[:, 1].reshape(STEP_K2 * HALF, MAXLAG)
        whole_re = jnp.concatenate(parts_re, axis=0)
        whole_im = jnp.concatenate(parts_im, axis=0)
        return (
            jnp.dot(whole_re, table_cos, preferred_element_type=f32),
            jnp.dot(whole_im, table_sin, preferred_element_type=f32),
        )

    @pl.when(step == 0)
    def _():
        even[...], odd[...] = products(True)

    @pl.when(step > 0)
    def _():
        part_even, part_odd = products(False)
        even[...] += part_even
        odd[...] += part_odd

    @pl.when(step == pl.num_programs(0) - 1)
    def _():
        early = (even[...] + odd[...]).astype(bf16)
        early = jnp.dot(early, turn_ref[...], preferred_element_type=f32)
        late = even[...] - odd[...]
        rows = sources * chans // len(outs)
        for i, out in enumerate(outs):
            here = slice(i * rows, (i + 1) * rows)
            out[:, :MAXLAG] = early[here].astype(out.dtype)
            out[:, MAXLAG:] = late[here].astype(out.dtype)


def correlate(near, swap, got, lags, part, dtypes):
    tab = tables()
    sources, outs = 16, len(dtypes)
    count = near.shape[1]
    steps = ROWS_B // STEP_K2
    rows = count * sources
    src_spec = pl.BlockSpec((STEP_K2, sources, 2 * HALF), lambda i: (i, part, 0))
    src_ratio = pl.BlockSpec((1, sources, 2 * HALF), lambda i: (ROWS_B, part, 0))
    chan_spec = pl.BlockSpec((STEP_K2, count, 2 * HALF), lambda i: (i, 1, 0))
    chan_ratio = pl.BlockSpec((1, count, 2 * HALF), lambda i: (ROWS_B, 1, 0))
    table = pl.BlockSpec((STEP_K2, 2, HALF, MAXLAG), lambda i: (i, 0, 0, 0))
    out_spec = pl.BlockSpec((rows // outs, LAGS), lambda i: (0, 0))
    return pl.pallas_call(
        correlate_kernel,
        grid=(steps,),
        in_specs=[src_spec, src_spec, src_ratio, src_ratio, chan_spec, chan_spec, chan_ratio, chan_ratio]
        + [table, pl.BlockSpec((MAXLAG, MAXLAG), lambda i: (0, 0))],
        out_specs=[out_spec] * outs,
        out_shape=[jax.ShapeDtypeStruct((rows // outs, LAGS), dtype) for dtype in dtypes],
        scratch_shapes=[
            pltpu.VMEM((rows, MAXLAG), jnp.float32),
            pltpu.VMEM((rows, MAXLAG), jnp.float32),
            pltpu.VMEM((2, sources, count, HALF), jnp.bfloat16),
            pltpu.VMEM((2, sources, count, HALF), jnp.bfloat16),
            pltpu.VMEM((2, STEP_K2, 2, sources, HALF), jnp.float32),
        ],
        compiler_params=pltpu.CompilerParams(vmem_limit_bytes=VMEM_LIMIT),
        cost_estimate=pl.CostEstimate(
            flops=4 * rows * SPAN * MAXLAG, bytes_accessed=8 * 1024 * 1024, transcendentals=0
        ),
        name="correlate",
    )(near, got, near, got, swap, got, swap, got, lags, tab["turn"])


def finish_kernel(own_ref, first_ref, second_ref, count_ref, out_ref):
    for at in range(0, LAGS, HALF):
        here = slice(at, at + HALF)
        total = own_ref[:, here] + first_ref[:, here].astype(jnp.float32)
        out_ref[:, here] = (total + second_ref[:, here].astype(jnp.float32)) / count_ref[...]


def finish(own, first, second, count):
    return pl.pallas_call(
        finish_kernel,
        out_shape=jax.ShapeDtypeStruct(own.shape, jnp.float32),
        compiler_params=pltpu.CompilerParams(vmem_limit_bytes=VMEM_LIMIT),
        name="finish",
    )(own, first, second, count)


def source_order(time_index, shape):
    row = lax.broadcasted_iota(jnp.int32, shape, 0)
    place = (row // 8) % 4
    parity = (time_index % 2 + row // 32) % 2
    near_by = jnp.where((place == 1) == (parity == 0), 3, 1)
    relative = jnp.where(place == 0, 2, jnp.where(place == 3, 0, near_by))
    z_hi = (time_index // 2 + relative) % 4
    return (2 * z_hi + parity) * 8 + row % 8


def body(record, fir_taps, sources, valid_mask):
    chan_count = lax.axis_size("chan")
    time_count = lax.axis_size("tm")
    _, channels, part_len = record.shape
    chan_local = channels // chan_count
    source_total = sources.shape[0]
    chan_index = lax.axis_index("chan")
    time_index = lax.axis_index("tm")
    first_chan = chan_index * chan_local

    sent = gather_rows(sources, record[0].T, chan_count)
    pieces = lax.all_to_all(sent, "chan", split_axis=0, concat_axis=0, tiled=True)

    toeplitz = toeplitz_of(fir_taps)
    valid_float = valid_mask.astype(jnp.float32)
    every_source = jnp.arange(source_total, dtype=jnp.int32)
    every_channel = jnp.arange(channels, dtype=jnp.int32)
    order = source_order(time_index, (source_total, 1))
    ordered = jnp.sum(jnp.where(order == every_source[None, :], sources[None, :], 0), axis=1)
    own = first_chan + jnp.arange(chan_local, dtype=jnp.int32)
    rows = jnp.concatenate([ordered, own])
    window_valid = lax.dynamic_index_in_dim(valid_float, time_index, 0, keepdims=False)
    mask = jnp.sum(jnp.where(rows[:, None] == every_channel[None, :], window_valid[None, :], 0.0), axis=1)
    mask = jnp.broadcast_to(mask[:, None], (rows.shape[0], HALF))
    chan_valid = lax.dynamic_slice_in_dim(valid_float, first_chan, chan_local, 1)
    rows_out = source_total // time_count
    own_sources = lax.dynamic_slice_in_dim(sources, time_index * rows_out, rows_out, 0)
    own_picker = (own_sources[:, None] == every_channel[None, :]).astype(jnp.float32)
    own_valid = jnp.dot(own_picker, valid_float.T, precision=lax.Precision.HIGHEST)
    pair_count = jnp.dot(own_valid, chan_valid, precision=lax.Precision.HIGHEST)

    third = source_total // 2
    swap = front(pieces, toeplitz, mask, third, 2 * third, third)
    got = lax.ppermute(swap, "tm", [(j, j ^ 1) for j in range(time_count)])
    near = front(pieces, toeplitz, mask, 0, third, third)

    def along(way, values):
        steps = [2 * way * (1 - 2 * (j % 2)) for j in range(time_count)]
        return lax.ppermute(values, "tm", [(j, (j + steps[j]) % time_count) for j in range(time_count)])

    bf16, f32 = jnp.bfloat16, jnp.float32
    lags = pltpu.with_memory_space_constraint(jnp.asarray(tables()["lags"]), pltpu.VMEM)
    far, second = correlate(near, swap, got, lags, 0, (bf16, bf16))
    far, second = along(1, far), along(-1, second)
    first, own_part = correlate(near, swap, got, lags, 1, (f32, f32))
    first = along(1, (first + far.astype(f32)).astype(bf16))
    count = jnp.maximum(pair_count, 1.0)[:, :, None]
    count = jnp.broadcast_to(count, count.shape[:2] + (HALF,)).reshape(rows_out * chan_local, HALF)
    stack = finish(own_part, first, second, count)
    return stack.reshape(rows_out, chan_local, LAGS)


def solution(mesh):
    return jax.shard_map(
        body,
        mesh=mesh,
        in_specs=(P("tm", None, "chan"), P(), P(), P()),
        out_specs=P("tm", "chan", None),
        check_vma=False,
    )
```

```python
import functools
import math

import jax
import jax.numpy as jnp
import numpy as np
from jax import lax
from jax.experimental import pallas as pl
from jax.experimental.pallas import tpu as pltpu
from jax.sharding import PartitionSpec as P

SPAN = 8192
SAMPLES = 7680
ROWS_B = 32
COLS_A = 256
HALF = 128
BAND = 128
MAXLAG = 256
LAGS = 512
TILE = 256
STEP_K2 = 16
ROW_STEP = 16
ROW_PART = 8
VMEM_LIMIT = 16 * 1024 * 1024
PLANES = ROWS_B + 1


def angle_tables(left, right, period):
    angles = (np.outer(left, right) % period) * (2.0 * math.pi / period)
    return np.cos(angles), np.sin(angles)


@functools.cache
def tables():
    b = np.arange(ROWS_B)
    a = np.arange(COLS_A)
    k1 = np.arange(HALF)
    cos_b, sin_b = angle_tables(b, b, ROWS_B)
    used = np.concatenate([cos_b, -sin_b], axis=0)[:, : SAMPLES // COLS_A]
    first = np.kron(used, np.eye(ROW_PART))
    twist = np.stack(angle_tables(b, a, SPAN)).astype(np.float32)
    cos_a, sin_a = angle_tables(a, k1, COLS_A)
    second = np.concatenate(
        [np.concatenate([cos_a, -sin_a], axis=1), np.concatenate([sin_a, cos_a], axis=1)], axis=0
    )
    bins = b[:, None] + ROWS_B * k1[None, :]
    shift = np.stack([np.cos(bins * math.pi / SPAN), np.sin(bins * math.pi / SPAN)])
    odd = 2 * np.arange(MAXLAG) + 1
    angles = (np.outer(bins.reshape(-1), odd) % (2 * SPAN)) * (math.pi / SPAN)
    scale = 1.0 / math.sqrt(SPAN)
    lag_cos = (np.cos(angles) * scale).reshape(ROWS_B, HALF, MAXLAG)
    lag_sin = (np.sin(angles) * scale).reshape(ROWS_B, HALF, MAXLAG)
    lag_sin[0, 0] = scale * (1 - 2 * (np.arange(MAXLAG) % 2))
    band = k1 // 4
    same = (band[:, None] == band[None, :]).astype(np.float32)
    lead = (k1 % 4 == 0)[:, None]
    following = (k1[:, None] == 4 * (band[None, :] + 1)).astype(np.float32)
    mirror_rest, mirror_edge = same, same * ~lead + following
    back = np.where(k1 % 4 == 0, np.maximum(k1 - 1, 0), k1)
    sums = np.concatenate(
        [
            np.concatenate([same, mirror_rest, mirror_rest[:, back]], axis=1),
            np.concatenate([same, mirror_edge, mirror_edge[:, back]], axis=1),
        ],
        axis=0,
    )
    nyquist = np.zeros((1, 3 * HALF), np.float32)
    nyquist[0, HALF + 124 : 2 * HALF] = 1.0
    nyquist[0, 2 * HALF + 125 :] = 1.0
    signs = (1.0 - 2.0 * (np.arange(COLS_A) % 2))[None].astype(np.float32)
    bf16 = jnp.bfloat16
    return dict(
        turn=np.eye(MAXLAG)[::-1].astype(bf16),
        products=np.concatenate(
            [np.pad(first, ((0, 0), (0, COLS_A - first.shape[1]))), second, sums[:, : 2 * HALF]]
            + [np.pad(sums[:, 2 * HALF :], ((0, 0), (0, HALF)))]
        ).astype(bf16),
        rotations=np.concatenate(
            [twist[0], twist[1], np.concatenate([shift[0], shift[1]], axis=1)]
            + [np.repeat(v, 8, axis=0) for v in (signs, nyquist[:, : 2 * HALF])]
            + [np.repeat(np.pad(nyquist[:, 2 * HALF :], ((0, 0), (0, HALF))), 8, axis=0)]
        ).astype(np.float32),
        lags=np.stack([lag_cos, lag_sin], axis=1).astype(bf16),
    )


def in_hbm(array):
    return pltpu.with_memory_space_constraint(array, pltpu.HBM)


def in_vmem(array):
    return pltpu.with_memory_space_constraint(jnp.asarray(array), pltpu.VMEM)


def toeplitz_kernel(taps_ref, *rest):
    out_ref = rest[-1]
    rows, width = out_ref.shape
    base = jnp.broadcast_to(taps_ref[...], (rows, taps_ref.shape[1]))
    turned = pltpu.roll(base, taps_ref.shape[1] - MAXLAG, 1, stride=1, stride_axis=0)
    out_ref[...] = turned[:, :width].astype(out_ref.dtype)


def toeplitz_of(fir_taps, *held):
    base = jnp.pad(fir_taps.astype(jnp.float32), (0, 1024 - fir_taps.shape[0]))[None, :]
    return pl.pallas_call(
        toeplitz_kernel,
        in_specs=[pl.BlockSpec(base.shape, lambda: (0, 0))] + [pl.BlockSpec(memory_space=pl.ANY)] * len(held),
        out_shape=jax.ShapeDtypeStruct((2 * TILE, TILE), jnp.bfloat16),
        compiler_params=pltpu.CompilerParams(vmem_limit_bytes=VMEM_LIMIT),
        name="toeplitz",
    )(base, *held)


def gather_kernel(sources_ref, record_ref, out_ref, picked):
    sources = sources_ref.shape[1]
    count, rows, _ = out_ref.shape
    own = rows - sources
    step = pl.program_id(0)
    turned = (((1,), (1,)), ((), ()))

    def pick(rows_wanted, values):
        channel = lax.broadcasted_iota(jnp.int32, (rows_wanted.shape[0], values.shape[1]), 1)
        picker = jnp.where(channel == rows_wanted, 1.0, 0.0).astype(jnp.bfloat16)
        rows_of = lax.dot_general(picker, values, turned, preferred_element_type=jnp.float32)
        return rows_of.astype(jnp.bfloat16)

    @pl.when(step == 0)
    def _():
        order = source_order(lax.axis_index("tm"), (sources, sources))
        lane = lax.broadcasted_iota(jnp.int32, (sources, sources), 1)
        channels = jnp.where(lane == order, sources_ref[...].astype(jnp.float32), 0.0)
        channels = jnp.sum(channels, axis=1, keepdims=True).astype(jnp.int32)
        picked[...] = pick(channels, record_ref[...])

    here = pl.ds(pl.multiple_of(step * (count * own), count * own), count * own)
    straight = lax.broadcasted_iota(jnp.int32, (count * own, 1), 0)
    mine = pick(straight, record_ref[:, here])
    for i in range(count):
        out_ref[i, :sources] = picked[...]
        out_ref[i, sources:] = mine[i * own : (i + 1) * own]


def gather_rows(sources, record, chan_count):
    length, channels = record.shape
    total = sources.shape[0]
    rows = total + channels // chan_count
    steps = 2
    return pl.pallas_call(
        gather_kernel,
        grid=(steps,),
        in_specs=[
            pl.BlockSpec((1, total), lambda i: (0, 0)),
            pl.BlockSpec((length, channels), lambda i: (0, 0)),
        ],
        out_specs=pl.BlockSpec((chan_count // steps, rows, length), lambda i: (i, 0, 0)),
        out_shape=jax.ShapeDtypeStruct((chan_count, rows, length), jnp.bfloat16),
        scratch_shapes=[pltpu.VMEM((total, length), jnp.bfloat16)],
        compiler_params=pltpu.CompilerParams(vmem_limit_bytes=VMEM_LIMIT),
        name="gather",
    )(in_hbm(sources[None, :]), in_hbm(record))


def front_kernel(rotated, pieces_ref, toeplitz_ref, products_ref, rotations_ref, mask_ref, out_ref, signal):
    count, rows, part = pieces_ref.shape
    length = count * part
    f32, bf16 = jnp.float32, jnp.bfloat16
    signal[:, :HALF] = jnp.zeros((rows, HALF), bf16)
    signal[:, HALF + length :] = jnp.zeros((rows, HALF), bf16)
    for i in range(count):
        signal[:, HALF + i * part : HALF + (i + 1) * part] = pieces_ref[i]
    tiles = jnp.concatenate(
        [signal[:, n * TILE : n * TILE + 2 * TILE] for n in range(length // TILE)], axis=0
    )
    made = jnp.dot(tiles, toeplitz_ref[...], preferred_element_type=f32)
    made = made.reshape(length // TILE, rows, TILE)
    zetas = []
    split = 2 * ROWS_B * ROW_PART
    for part in range(rows // ROW_PART):
        filtered = made[:, part * ROW_PART : (part + 1) * ROW_PART].reshape(-1, TILE).astype(bf16)
        zetas.append(jnp.dot(products_ref[:split, : filtered.shape[0]], filtered, preferred_element_type=f32))
    turned_re, turned_im = [], []
    for k2 in range(ROWS_B):
        cos = jnp.broadcast_to(rotations_ref[k2 : k2 + 1, :], (ROW_PART, COLS_A))
        sin = jnp.broadcast_to(rotations_ref[ROWS_B + k2 : ROWS_B + k2 + 1, :], (ROW_PART, COLS_A))
        for zeta in zetas:
            zeta_re = zeta[k2 * ROW_PART : (k2 + 1) * ROW_PART]
            zeta_im = zeta[(ROWS_B + k2) * ROW_PART : (ROWS_B + k2 + 1) * ROW_PART]
            turned_re.append(zeta_re * cos + zeta_im * sin)
            turned_im.append(zeta_im * cos - zeta_re * sin)
    twisted_re = jnp.concatenate(turned_re, axis=0).astype(bf16)
    twisted_im = jnp.concatenate(turned_im, axis=0).astype(bf16)
    nyquist = jnp.sum(twisted_re[:rows].astype(f32) * rotations_ref[3 * ROWS_B : 3 * ROWS_B + 1], axis=1, keepdims=True)
    twisted = jnp.concatenate([twisted_re, twisted_im], axis=1)
    spectrum = jnp.dot(twisted, products_ref[split : split + 2 * COLS_A], preferred_element_type=f32)
    re, im = spectrum[:, :HALF], spectrum[:, HALF:]

    size = jnp.sqrt(re * re + im * im)
    rest = jnp.sum(size[rows:].reshape(ROWS_B - 1, rows, HALF), axis=0)
    both = jnp.concatenate([rest, size[:rows]], axis=1)
    high = both.astype(bf16)
    left = both - high.astype(f32)
    middle = left.astype(bf16)
    low = (left - middle.astype(f32)).astype(bf16)
    split += 2 * COLS_A
    parts = jnp.concatenate([high, middle, low], axis=0)
    parts = [
        jnp.dot(parts, products_ref[at : at + 2 * HALF], preferred_element_type=f32)
        for at in (split, split + 2 * HALF)
    ]
    parts = jnp.concatenate([parts[0], parts[1][:, :HALF]], axis=1)
    sums = parts[:rows] + parts[rows : 2 * rows] + parts[2 * rows :]
    at = 3 * ROWS_B + 8
    first_part, last_part = rotations_ref[at : at + 1], rotations_ref[at + 8 : at + 9, :HALF]
    sums = sums + jnp.abs(nyquist) * jnp.concatenate([first_part, last_part], axis=1)
    levels = sums * (1.0 / BAND) + 1e-05
    level, mirror, mirror_lead = levels[:, :HALF], levels[:, HALF : 2 * HALF], levels[:, 2 * HALF :]
    lane = lax.broadcasted_iota(jnp.int32, (rows, HALF), 1)
    mask = mask_ref[...]
    gain = mask / level
    white_nyquist = mask[:, :1] * nyquist / mirror[:, HALF - 1 :]
    ratio = (level / mirror).astype(bf16)
    ratio_lead = jnp.where(lane == 0, 0.0, level / mirror_lead).astype(bf16)

    def write(out_ref, rotate):
        for k2 in range(ROWS_B):
            here = slice(k2 * rows, (k2 + 1) * rows)
            white_re, white_im = re[here] * gain, im[here] * gain
            if rotate:
                turns = rotations_ref[2 * ROWS_B + k2 : 2 * ROWS_B + k2 + 1, :]
                turn_cos = jnp.broadcast_to(turns[:, :HALF], (rows, HALF))
                turn_sin = jnp.broadcast_to(turns[:, HALF:], (rows, HALF))
                white_re, white_im = (
                    white_re * turn_cos + white_im * turn_sin,
                    white_im * turn_cos - white_re * turn_sin,
                )
            if k2 == 0:
                white_im = jnp.where(lane == 0, white_nyquist, white_im)
            out_ref[k2, :, :HALF] = white_re.astype(bf16)
            out_ref[k2, :, HALF:] = white_im.astype(bf16)
        out_ref[ROWS_B, :, :HALF] = ratio
        out_ref[ROWS_B, :, HALF:] = ratio_lead

    is_source = pl.program_id(0) < rotated
    pl.when(is_source)(lambda: write(out_ref, True))
    pl.when(jnp.logical_not(is_source))(lambda: write(out_ref, False))


def front(pieces, toeplitz, products, rotations, mask, start, rows, rotated):
    count, _, part = pieces.shape
    start = start // ROW_STEP

    def whole(array):
        return pl.BlockSpec(array.shape, lambda i, rank=array.ndim: (0,) * rank)

    return pl.pallas_call(
        functools.partial(front_kernel, rotated // ROW_STEP),
        grid=(rows // ROW_STEP,),
        in_specs=[
            pl.BlockSpec((count, ROW_STEP, part), lambda i: (0, start + i, 0)),
            whole(toeplitz),
            whole(products),
            whole(rotations),
            pl.BlockSpec((ROW_STEP, HALF), lambda i: (start + i, 0)),
        ],
        out_specs=pl.BlockSpec((PLANES, ROW_STEP, 2 * HALF), lambda i: (0, i, 0)),
        out_shape=jax.ShapeDtypeStruct((PLANES, rows, 2 * HALF), jnp.bfloat16),
        scratch_shapes=[pltpu.VMEM((ROW_STEP, count * part + 2 * HALF), jnp.bfloat16)],
        compiler_params=pltpu.CompilerParams(vmem_limit_bytes=VMEM_LIMIT),
        cost_estimate=pl.CostEstimate(flops=rows * 110_000_000, bytes_accessed=4_000_000, transcendentals=0),
        name="front",
    )(in_vmem(pieces), in_vmem(toeplitz), products, rotations, mask)


def correlate_kernel(src0, src1, sratio0, sratio1, chan0, chan1, cratio0, cratio1, lags_ref, turn_ref,
                     *rest):
    outs, (even, odd, weight, lead_weight, src_wide) = rest[:-5], rest[-5:]
    step = pl.program_id(0)
    chans = chan0.shape[1]
    sources = src0.shape[1]
    f32, bf16 = jnp.float32, jnp.bfloat16
    srcs, chan_refs = (src0, src1), (chan0, chan1)

    def spread(w, j, s, h):
        return jnp.broadcast_to(src_wide[w, j, h, pl.ds(s, 1), :], (chans, HALF)).astype(bf16)

    @pl.when(step == 0)
    def _():
        for w, (sratio, cratio) in enumerate(((sratio0, cratio0), (sratio1, cratio1))):
            for h in range(2):
                src_wide[w, 0, h] = sratio[0, :, h * HALF : (h + 1) * HALF].astype(f32)
            for s in range(sources):
                weight[w, s] = 1.0 + cratio[0, :, :HALF] * spread(w, 0, s, 0)
                lead_weight[w, s] = 1.0 + cratio[0, :, HALF:] * spread(w, 0, s, 1)

    for w in range(2):
        for h in range(2):
            src_wide[w, :, h] = srcs[w][:, :, h * HALF : (h + 1) * HALF].astype(f32)

    def products(with_lead):
        parts_re, parts_im = [], []
        lane = lax.broadcasted_iota(jnp.int32, (chans, HALF), 1)
        keep = jnp.where(lane == 0, 0.0, 1.0).astype(bf16)
        only = jnp.where(lane == 0, 1.0, 0.0).astype(bf16)
        for s in range(sources):
            row_re, row_im = [], []
            for j in range(STEP_K2):
                total_re = total_im = None
                for w in range(2):
                    chan_re, chan_im = chan_refs[w][j, :, :HALF], chan_refs[w][j, :, HALF:]
                    src_re, src_im = spread(w, j, s, 0), spread(w, j, s, 1)
                    same_re, same_im = src_re * chan_re, src_im * chan_im
                    mixed = src_im * chan_re - src_re * chan_im
                    if with_lead and j == 0:
                        scale = lead_weight[w, s]
                        part_re = (same_re + same_im * keep) * scale
                        part_im = (mixed * keep - same_im * only) * scale
                    else:
                        scale = weight[w, s]
                        part_re = (same_re + same_im) * scale
                        part_im = mixed * scale
                    total_re = part_re if w == 0 else total_re + part_re
                    total_im = part_im if w == 0 else total_im + part_im
                row_re.append(total_re)
                row_im.append(total_im)
            parts_re.append(jnp.concatenate(row_re, axis=1))
            parts_im.append(jnp.concatenate(row_im, axis=1))
        table_cos = lags_ref[:, 0].reshape(STEP_K2 * HALF, MAXLAG)
        table_sin = lags_ref[:, 1].reshape(STEP_K2 * HALF, MAXLAG)
        whole_re = jnp.concatenate(parts_re, axis=0)
        whole_im = jnp.concatenate(parts_im, axis=0)
        return (
            jnp.dot(whole_re, table_cos, preferred_element_type=f32),
            jnp.dot(whole_im, table_sin, preferred_element_type=f32),
        )

    @pl.when(step == 0)
    def _():
        even[...], odd[...] = products(True)

    @pl.when(step > 0)
    def _():
        part_even, part_odd = products(False)
        even[...] += part_even
        odd[...] += part_odd

    @pl.when(step == pl.num_programs(0) - 1)
    def _():
        early = (even[...] + odd[...]).astype(bf16)
        early = jnp.dot(early, turn_ref[...], preferred_element_type=f32)
        late = even[...] - odd[...]
        rows = sources * chans // len(outs)
        for i, out in enumerate(outs):
            here = slice(i * rows, (i + 1) * rows)
            out[:, :MAXLAG] = early[here].astype(out.dtype)
            out[:, MAXLAG:] = late[here].astype(out.dtype)


def correlate(near, swap, got, lags, part, dtypes):
    tab = tables()
    sources, outs = 16, len(dtypes)
    count = near.shape[1]
    steps = ROWS_B // STEP_K2
    rows = count * sources
    src_spec = pl.BlockSpec((STEP_K2, sources, 2 * HALF), lambda i: (i, part, 0))
    src_ratio = pl.BlockSpec((1, sources, 2 * HALF), lambda i: (ROWS_B, part, 0))
    chan_spec = pl.BlockSpec((STEP_K2, count, 2 * HALF), lambda i: (i, 1, 0))
    chan_ratio = pl.BlockSpec((1, count, 2 * HALF), lambda i: (ROWS_B, 1, 0))
    table = pl.BlockSpec((STEP_K2, 2, HALF, MAXLAG), lambda i: (i, 0, 0, 0))
    out_spec = pl.BlockSpec((rows // outs, LAGS), lambda i: (0, 0))
    return pl.pallas_call(
        correlate_kernel,
        grid=(steps,),
        in_specs=[src_spec, src_spec, src_ratio, src_ratio, chan_spec, chan_spec, chan_ratio, chan_ratio]
        + [table, pl.BlockSpec((MAXLAG, MAXLAG), lambda i: (0, 0))],
        out_specs=[out_spec] * outs,
        out_shape=[jax.ShapeDtypeStruct((rows // outs, LAGS), dtype) for dtype in dtypes],
        scratch_shapes=[
            pltpu.VMEM((rows, MAXLAG), jnp.float32),
            pltpu.VMEM((rows, MAXLAG), jnp.float32),
            pltpu.VMEM((2, sources, count, HALF), jnp.bfloat16),
            pltpu.VMEM((2, sources, count, HALF), jnp.bfloat16),
            pltpu.VMEM((2, STEP_K2, 2, sources, HALF), jnp.float32),
        ],
        compiler_params=pltpu.CompilerParams(vmem_limit_bytes=VMEM_LIMIT),
        cost_estimate=pl.CostEstimate(
            flops=4 * rows * SPAN * MAXLAG, bytes_accessed=8 * 1024 * 1024, transcendentals=0
        ),
        name="correlate",
    )(near, got, near, got, swap, got, swap, got, lags, tab["turn"])


def finish_kernel(own_ref, first_ref, second_ref, count_ref, out_ref):
    for at in range(0, LAGS, HALF):
        here = slice(at, at + HALF)
        total = own_ref[:, here] + first_ref[:, here].astype(jnp.float32)
        out_ref[:, here] = (total + second_ref[:, here].astype(jnp.float32)) / count_ref[...]


def finish(own, first, second, count):
    return pl.pallas_call(
        finish_kernel,
        out_shape=jax.ShapeDtypeStruct(own.shape, jnp.float32),
        compiler_params=pltpu.CompilerParams(vmem_limit_bytes=VMEM_LIMIT),
        name="finish",
    )(own, first, second, count)


def source_order(time_index, shape):
    row = lax.broadcasted_iota(jnp.int32, shape, 0)
    place = (row // 8) % 4
    parity = (time_index % 2 + row // 32) % 2
    near_by = jnp.where((place == 1) == (parity == 0), 1, 3)
    relative = jnp.where(place == 0, 2, jnp.where(place == 3, 0, near_by))
    z_hi = (time_index // 2 + relative) % 4
    return (2 * z_hi + parity) * 8 + row % 8


def body(record, fir_taps, sources, valid_mask):
    chan_count = lax.axis_size("chan")
    time_count = lax.axis_size("tm")
    _, channels, part_len = record.shape
    chan_local = channels // chan_count
    source_total = sources.shape[0]
    chan_index = lax.axis_index("chan")
    time_index = lax.axis_index("tm")
    first_chan = chan_index * chan_local

    sent = gather_rows(sources, record[0].T, chan_count)
    pieces = lax.all_to_all(sent, "chan", split_axis=0, concat_axis=0, tiled=True)

    tab = tables()
    products, rotations = in_vmem(tab["products"]), in_vmem(tab["rotations"])
    lags = in_vmem(tab["lags"])
    toeplitz = toeplitz_of(fir_taps, products, rotations)
    valid_float = valid_mask.astype(jnp.float32)
    every_source = jnp.arange(source_total, dtype=jnp.int32)
    every_channel = jnp.arange(channels, dtype=jnp.int32)
    order = source_order(time_index, (source_total, 1))
    ordered = jnp.sum(jnp.where(order == every_source[None, :], sources[None, :], 0), axis=1)
    own = first_chan + jnp.arange(chan_local, dtype=jnp.int32)
    rows = jnp.concatenate([ordered, own])
    window_valid = lax.dynamic_index_in_dim(valid_float, time_index, 0, keepdims=False)
    mask = jnp.sum(jnp.where(rows[:, None] == every_channel[None, :], window_valid[None, :], 0.0), axis=1)
    mask = jnp.broadcast_to(mask[:, None], (rows.shape[0], HALF))
    chan_valid = lax.dynamic_slice_in_dim(valid_float, first_chan, chan_local, 1)
    rows_out = source_total // time_count
    own_sources = lax.dynamic_slice_in_dim(sources, time_index * rows_out, rows_out, 0)
    own_picker = (own_sources[:, None] == every_channel[None, :]).astype(jnp.float32)
    own_valid = jnp.dot(own_picker, valid_float.T, precision=lax.Precision.HIGHEST)
    pair_count = jnp.dot(own_valid, chan_valid, precision=lax.Precision.HIGHEST)

    third = source_total // 2
    swap = front(pieces, toeplitz, products, rotations, mask, third, 2 * third, third)
    got = lax.ppermute(swap, "tm", [(j, j ^ 1) for j in range(time_count)])
    near = front(pieces, toeplitz, products, rotations, mask, 0, third, third)

    def along(way, values):
        steps = [2 * way * (1 - 2 * (j % 2)) for j in range(time_count)]
        return lax.ppermute(values, "tm", [(j, (j + steps[j]) % time_count) for j in range(time_count)])

    bf16, f32 = jnp.bfloat16, jnp.float32
    far, first = correlate(near, swap, got, lags, 0, (bf16, f32))
    far = along(1, far)
    second, own_part = correlate(near, swap, got, lags, 1, (bf16, f32))
    first = along(1, (first + far.astype(f32)).astype(bf16))
    second = along(-1, second)
    count = jnp.maximum(pair_count, 1.0)[:, :, None]
    count = jnp.broadcast_to(count, count.shape[:2] + (HALF,)).reshape(rows_out * chan_local, HALF)
    stack = finish(own_part, first, second, count)
    return stack.reshape(rows_out, chan_local, LAGS)


def solution(mesh):
    return jax.shard_map(
        body,
        mesh=mesh,
        in_specs=(P("tm", None, "chan"), P(), P(), P()),
        out_specs=P("tm", "chan", None),
        check_vma=False,
    )
```

```python
import functools
import math

import jax
import jax.numpy as jnp
import numpy as np
from jax import lax
from jax.experimental import pallas as pl
from jax.experimental.pallas import tpu as pltpu
from jax.sharding import PartitionSpec as P

SPAN = 8192
SAMPLES = 7680
ROWS_B = 32
COLS_A = 256
HALF = 128
BAND = 128
MAXLAG = 256
LAGS = 512
TILE = 256
STEP_K2 = 16
ROW_STEP = 32
ROW_PART = 8
VMEM_LIMIT = 16 * 1024 * 1024
PLANES = ROWS_B + 1


def angle_tables(left, right, period):
    angles = (np.outer(left, right) % period) * (2.0 * math.pi / period)
    return np.cos(angles), np.sin(angles)


@functools.cache
def tables():
    b = np.arange(ROWS_B)
    a = np.arange(COLS_A)
    k1 = np.arange(HALF)
    cos_b, sin_b = angle_tables(b, b, ROWS_B)
    used = np.concatenate([cos_b, -sin_b], axis=0)[:, : SAMPLES // COLS_A]
    first = np.kron(used, np.eye(ROW_PART))
    twist = np.stack(angle_tables(b, a, SPAN)).astype(np.float32)
    cos_a, sin_a = angle_tables(a, k1, COLS_A)
    second = np.concatenate(
        [np.concatenate([cos_a, -sin_a], axis=1), np.concatenate([sin_a, cos_a], axis=1)], axis=0
    )
    bins = b[:, None] + ROWS_B * k1[None, :]
    shift = np.stack([np.cos(bins * math.pi / SPAN), np.sin(bins * math.pi / SPAN)])
    odd = 2 * np.arange(MAXLAG) + 1
    angles = (np.outer(bins.reshape(-1), odd) % (2 * SPAN)) * (math.pi / SPAN)
    scale = 1.0 / math.sqrt(SPAN)
    lag_cos = (np.cos(angles) * scale).reshape(ROWS_B, HALF, MAXLAG)
    lag_sin = (np.sin(angles) * scale).reshape(ROWS_B, HALF, MAXLAG)
    lag_sin[0, 0] = scale * (1 - 2 * (np.arange(MAXLAG) % 2))
    band = k1 // 4
    same = (band[:, None] == band[None, :]).astype(np.float32)
    lead = (k1 % 4 == 0)[:, None]
    following = (k1[:, None] == 4 * (band[None, :] + 1)).astype(np.float32)
    mirror_rest, mirror_edge = same, same * ~lead + following
    back = np.where(k1 % 4 == 0, np.maximum(k1 - 1, 0), k1)
    sums = np.concatenate(
        [
            np.concatenate([same, mirror_rest, mirror_rest[:, back]], axis=1),
            np.concatenate([same, mirror_edge, mirror_edge[:, back]], axis=1),
        ],
        axis=0,
    )
    nyquist = np.zeros((1, 3 * HALF), np.float32)
    nyquist[0, HALF + 124 : 2 * HALF] = 1.0
    nyquist[0, 2 * HALF + 125 :] = 1.0
    signs = (1.0 - 2.0 * (np.arange(COLS_A) % 2))[None].astype(np.float32)
    bf16 = jnp.bfloat16
    return dict(
        turn=np.eye(MAXLAG)[::-1].astype(bf16),
        products=np.concatenate(
            [np.pad(first, ((0, 0), (0, COLS_A - first.shape[1]))), second, sums[:, : 2 * HALF]]
            + [np.pad(sums[:, 2 * HALF :], ((0, 0), (0, HALF)))]
        ).astype(bf16),
        rotations=np.concatenate(
            [twist[0], twist[1], np.concatenate([shift[0], shift[1]], axis=1)]
            + [np.repeat(v, 8, axis=0) for v in (signs, nyquist[:, : 2 * HALF])]
            + [np.repeat(np.pad(nyquist[:, 2 * HALF :], ((0, 0), (0, HALF))), 8, axis=0)]
        ).astype(np.float32),
        lags=np.stack([lag_cos, lag_sin], axis=1).astype(bf16),
    )


def in_hbm(array):
    return pltpu.with_memory_space_constraint(array, pltpu.HBM)


def in_vmem(array):
    return pltpu.with_memory_space_constraint(jnp.asarray(array), pltpu.VMEM)


def toeplitz_kernel(taps_ref, *rest):
    out_ref = rest[-1]
    rows, width = out_ref.shape
    base = jnp.broadcast_to(taps_ref[...], (rows, taps_ref.shape[1]))
    turned = pltpu.roll(base, taps_ref.shape[1] - MAXLAG, 1, stride=1, stride_axis=0)
    out_ref[...] = turned[:, :width].astype(out_ref.dtype)


def toeplitz_of(fir_taps, *held):
    base = jnp.pad(fir_taps.astype(jnp.float32), (0, 1024 - fir_taps.shape[0]))[None, :]
    return pl.pallas_call(
        toeplitz_kernel,
        in_specs=[pl.BlockSpec(base.shape, lambda: (0, 0))] + [pl.BlockSpec(memory_space=pl.ANY)] * len(held),
        out_shape=jax.ShapeDtypeStruct((2 * TILE, TILE), jnp.bfloat16),
        compiler_params=pltpu.CompilerParams(vmem_limit_bytes=VMEM_LIMIT),
        name="toeplitz",
    )(base, *held)


def gather_kernel(sources_ref, record_ref, out_ref, picked):
    sources = sources_ref.shape[1]
    count, rows, _ = out_ref.shape
    own = rows - sources
    step = pl.program_id(0)
    turned = (((1,), (1,)), ((), ()))

    def pick(rows_wanted, values):
        channel = lax.broadcasted_iota(jnp.int32, (rows_wanted.shape[0], values.shape[1]), 1)
        picker = jnp.where(channel == rows_wanted, 1.0, 0.0).astype(jnp.bfloat16)
        rows_of = lax.dot_general(picker, values, turned, preferred_element_type=jnp.float32)
        return rows_of.astype(jnp.bfloat16)

    @pl.when(step == 0)
    def _():
        order = source_order(lax.axis_index("tm"), (sources, sources))
        lane = lax.broadcasted_iota(jnp.int32, (sources, sources), 1)
        channels = jnp.where(lane == order, sources_ref[...].astype(jnp.float32), 0.0)
        channels = jnp.sum(channels, axis=1, keepdims=True).astype(jnp.int32)
        picked[...] = pick(channels, record_ref[...])

    here = pl.ds(pl.multiple_of(step * (count * own), count * own), count * own)
    straight = lax.broadcasted_iota(jnp.int32, (count * own, 1), 0)
    mine = pick(straight, record_ref[:, here])
    for i in range(count):
        out_ref[i, :sources] = picked[...]
        out_ref[i, sources:] = mine[i * own : (i + 1) * own]


def gather_rows(sources, record, chan_count):
    length, channels = record.shape
    total = sources.shape[0]
    rows = total + channels // chan_count
    steps = 2
    return pl.pallas_call(
        gather_kernel,
        grid=(steps,),
        in_specs=[
            pl.BlockSpec((1, total), lambda i: (0, 0)),
            pl.BlockSpec((length, channels), lambda i: (0, 0)),
        ],
        out_specs=pl.BlockSpec((chan_count // steps, rows, length), lambda i: (i, 0, 0)),
        out_shape=jax.ShapeDtypeStruct((chan_count, rows, length), jnp.bfloat16),
        scratch_shapes=[pltpu.VMEM((total, length), jnp.bfloat16)],
        compiler_params=pltpu.CompilerParams(vmem_limit_bytes=VMEM_LIMIT),
        name="gather",
    )(in_hbm(sources[None, :]), in_hbm(record))


def front_kernel(rotated, pieces_ref, toeplitz_ref, products_ref, rotations_ref, mask_ref, out_ref, signal):
    count, rows, part = pieces_ref.shape
    length = count * part
    f32, bf16 = jnp.float32, jnp.bfloat16
    signal[:, :HALF] = jnp.zeros((rows, HALF), bf16)
    signal[:, HALF + length :] = jnp.zeros((rows, HALF), bf16)
    for i in range(count):
        signal[:, HALF + i * part : HALF + (i + 1) * part] = pieces_ref[i]
    tiles = jnp.concatenate(
        [signal[:, n * TILE : n * TILE + 2 * TILE] for n in range(length // TILE)], axis=0
    )
    made = jnp.dot(tiles, toeplitz_ref[...], preferred_element_type=f32)
    made = made.reshape(length // TILE, rows, TILE)
    zetas = []
    split = 2 * ROWS_B * ROW_PART
    for part in range(rows // ROW_PART):
        filtered = made[:, part * ROW_PART : (part + 1) * ROW_PART].reshape(-1, TILE).astype(bf16)
        zetas.append(jnp.dot(products_ref[:split, : filtered.shape[0]], filtered, preferred_element_type=f32))
    turned_re, turned_im = [], []
    for k2 in range(ROWS_B):
        cos = jnp.broadcast_to(rotations_ref[k2 : k2 + 1, :], (ROW_PART, COLS_A))
        sin = jnp.broadcast_to(rotations_ref[ROWS_B + k2 : ROWS_B + k2 + 1, :], (ROW_PART, COLS_A))
        for zeta in zetas:
            zeta_re = zeta[k2 * ROW_PART : (k2 + 1) * ROW_PART]
            zeta_im = zeta[(ROWS_B + k2) * ROW_PART : (ROWS_B + k2 + 1) * ROW_PART]
            turned_re.append(zeta_re * cos + zeta_im * sin)
            turned_im.append(zeta_im * cos - zeta_re * sin)
    twisted_re = jnp.concatenate(turned_re, axis=0).astype(bf16)
    twisted_im = jnp.concatenate(turned_im, axis=0).astype(bf16)
    nyquist = jnp.sum(twisted_re[:rows].astype(f32) * rotations_ref[3 * ROWS_B : 3 * ROWS_B + 1], axis=1, keepdims=True)
    twisted = jnp.concatenate([twisted_re, twisted_im], axis=1)
    spectrum = jnp.dot(twisted, products_ref[split : split + 2 * COLS_A], preferred_element_type=f32)
    re, im = spectrum[:, :HALF], spectrum[:, HALF:]

    size = jnp.sqrt(re * re + im * im)
    rest = jnp.sum(size[rows:].reshape(ROWS_B - 1, rows, HALF), axis=0)
    both = jnp.concatenate([rest, size[:rows]], axis=1)
    high = both.astype(bf16)
    left = both - high.astype(f32)
    middle = left.astype(bf16)
    low = (left - middle.astype(f32)).astype(bf16)
    split += 2 * COLS_A
    parts = jnp.concatenate([high, middle, low], axis=0)
    parts = [
        jnp.dot(parts, products_ref[at : at + 2 * HALF], preferred_element_type=f32)
        for at in (split, split + 2 * HALF)
    ]
    parts = jnp.concatenate([parts[0], parts[1][:, :HALF]], axis=1)
    sums = parts[:rows] + parts[rows : 2 * rows] + parts[2 * rows :]
    at = 3 * ROWS_B + 8
    first_part, last_part = rotations_ref[at : at + 1], rotations_ref[at + 8 : at + 9, :HALF]
    sums = sums + jnp.abs(nyquist) * jnp.concatenate([first_part, last_part], axis=1)
    levels = sums * (1.0 / BAND) + 1e-05
    level, mirror, mirror_lead = levels[:, :HALF], levels[:, HALF : 2 * HALF], levels[:, 2 * HALF :]
    lane = lax.broadcasted_iota(jnp.int32, (rows, HALF), 1)
    mask = mask_ref[...]
    gain = mask / level
    white_nyquist = mask[:, :1] * nyquist / mirror[:, HALF - 1 :]
    ratio = (level / mirror).astype(bf16)
    ratio_lead = jnp.where(lane == 0, 0.0, level / mirror_lead).astype(bf16)

    def write(out_ref, rotate):
        for k2 in range(ROWS_B):
            here = slice(k2 * rows, (k2 + 1) * rows)
            white_re, white_im = re[here] * gain, im[here] * gain
            if rotate:
                turns = rotations_ref[2 * ROWS_B + k2 : 2 * ROWS_B + k2 + 1, :]
                turn_cos = jnp.broadcast_to(turns[:, :HALF], (rows, HALF))
                turn_sin = jnp.broadcast_to(turns[:, HALF:], (rows, HALF))
                white_re, white_im = (
                    white_re * turn_cos + white_im * turn_sin,
                    white_im * turn_cos - white_re * turn_sin,
                )
            if k2 == 0:
                white_im = jnp.where(lane == 0, white_nyquist, white_im)
            out_ref[k2, :, :HALF] = white_re.astype(bf16)
            out_ref[k2, :, HALF:] = white_im.astype(bf16)
        out_ref[ROWS_B, :, :HALF] = ratio
        out_ref[ROWS_B, :, HALF:] = ratio_lead

    is_source = pl.program_id(0) < rotated
    pl.when(is_source)(lambda: write(out_ref, True))
    pl.when(jnp.logical_not(is_source))(lambda: write(out_ref, False))


def front(pieces, toeplitz, products, rotations, mask, start, rows, rotated):
    count, _, part = pieces.shape
    start = start // ROW_STEP

    def whole(array):
        return pl.BlockSpec(array.shape, lambda i, rank=array.ndim: (0,) * rank)

    return pl.pallas_call(
        functools.partial(front_kernel, rotated // ROW_STEP),
        grid=(rows // ROW_STEP,),
        in_specs=[
            pl.BlockSpec((count, ROW_STEP, part), lambda i: (0, start + i, 0)),
            whole(toeplitz),
            whole(products),
            whole(rotations),
            pl.BlockSpec((ROW_STEP, HALF), lambda i: (start + i, 0)),
        ],
        out_specs=pl.BlockSpec((PLANES, ROW_STEP, 2 * HALF), lambda i: (0, i, 0)),
        out_shape=jax.ShapeDtypeStruct((PLANES, rows, 2 * HALF), jnp.bfloat16),
        scratch_shapes=[pltpu.VMEM((ROW_STEP, count * part + 2 * HALF), jnp.bfloat16)],
        compiler_params=pltpu.CompilerParams(vmem_limit_bytes=VMEM_LIMIT),
        cost_estimate=pl.CostEstimate(flops=rows * 110_000_000, bytes_accessed=4_000_000, transcendentals=0),
        name="front",
    )(in_vmem(pieces), in_vmem(toeplitz), products, rotations, mask)


def correlate_kernel(src0, src1, sratio0, sratio1, chan0, chan1, cratio0, cratio1, lags_ref, turn_ref,
                     *rest):
    outs, (even, odd, weight, lead_weight, src_wide) = rest[:-5], rest[-5:]
    step = pl.program_id(0)
    chans = chan0.shape[1]
    sources = src0.shape[1]
    f32, bf16 = jnp.float32, jnp.bfloat16
    srcs, chan_refs = (src0, src1), (chan0, chan1)

    def spread(w, j, s, h):
        return jnp.broadcast_to(src_wide[w, j, h, pl.ds(s, 1), :], (chans, HALF)).astype(bf16)

    @pl.when(step == 0)
    def _():
        for w, (sratio, cratio) in enumerate(((sratio0, cratio0), (sratio1, cratio1))):
            for h in range(2):
                src_wide[w, 0, h] = sratio[0, :, h * HALF : (h + 1) * HALF].astype(f32)
            for s in range(sources):
                weight[w, s] = 1.0 + cratio[0, :, :HALF] * spread(w, 0, s, 0)
                lead_weight[w, s] = 1.0 + cratio[0, :, HALF:] * spread(w, 0, s, 1)

    for w in range(2):
        for h in range(2):
            src_wide[w, :, h] = srcs[w][:, :, h * HALF : (h + 1) * HALF].astype(f32)

    def products(with_lead):
        parts_re, parts_im = [], []
        lane = lax.broadcasted_iota(jnp.int32, (chans, HALF), 1)
        keep = jnp.where(lane == 0, 0.0, 1.0).astype(bf16)
        only = jnp.where(lane == 0, 1.0, 0.0).astype(bf16)
        for s in range(sources):
            row_re, row_im = [], []
            for j in range(STEP_K2):
                total_re = total_im = None
                for w in range(2):
                    chan_re, chan_im = chan_refs[w][j, :, :HALF], chan_refs[w][j, :, HALF:]
                    src_re, src_im = spread(w, j, s, 0), spread(w, j, s, 1)
                    same_re, same_im = src_re * chan_re, src_im * chan_im
                    mixed = src_im * chan_re - src_re * chan_im
                    if with_lead and j == 0:
                        scale = lead_weight[w, s]
                        part_re = (same_re + same_im * keep) * scale
                        part_im = (mixed * keep - same_im * only) * scale
                    else:
                        scale = weight[w, s]
                        part_re = (same_re + same_im) * scale
                        part_im = mixed * scale
                    total_re = part_re if w == 0 else total_re + part_re
                    total_im = part_im if w == 0 else total_im + part_im
                row_re.append(total_re)
                row_im.append(total_im)
            parts_re.append(jnp.concatenate(row_re, axis=1))
            parts_im.append(jnp.concatenate(row_im, axis=1))
        table_cos = lags_ref[:, 0].reshape(STEP_K2 * HALF, MAXLAG)
        table_sin = lags_ref[:, 1].reshape(STEP_K2 * HALF, MAXLAG)
        whole_re = jnp.concatenate(parts_re, axis=0)
        whole_im = jnp.concatenate(parts_im, axis=0)
        return (
            jnp.dot(whole_re, table_cos, preferred_element_type=f32),
            jnp.dot(whole_im, table_sin, preferred_element_type=f32),
        )

    @pl.when(step == 0)
    def _():
        even[...], odd[...] = products(True)

    @pl.when(step > 0)
    def _():
        part_even, part_odd = products(False)
        even[...] += part_even
        odd[...] += part_odd

    @pl.when(step == pl.num_programs(0) - 1)
    def _():
        early = (even[...] + odd[...]).astype(bf16)
        early = jnp.dot(early, turn_ref[...], preferred_element_type=f32)
        late = even[...] - odd[...]
        rows = sources * chans // len(outs)
        for i, out in enumerate(outs):
            here = slice(i * rows, (i + 1) * rows)
            out[:, :MAXLAG] = early[here].astype(out.dtype)
            out[:, MAXLAG:] = late[here].astype(out.dtype)


def correlate(near, swap, got, lags, part, dtypes):
    tab = tables()
    sources, outs = 16, len(dtypes)
    count = near.shape[1]
    steps = ROWS_B // STEP_K2
    rows = count * sources
    src_spec = pl.BlockSpec((STEP_K2, sources, 2 * HALF), lambda i: (i, part, 0))
    src_ratio = pl.BlockSpec((1, sources, 2 * HALF), lambda i: (ROWS_B, part, 0))
    chan_spec = pl.BlockSpec((STEP_K2, count, 2 * HALF), lambda i: (i, 1, 0))
    chan_ratio = pl.BlockSpec((1, count, 2 * HALF), lambda i: (ROWS_B, 1, 0))
    table = pl.BlockSpec((STEP_K2, 2, HALF, MAXLAG), lambda i: (i, 0, 0, 0))
    out_spec = pl.BlockSpec((rows // outs, LAGS), lambda i: (0, 0))
    return pl.pallas_call(
        correlate_kernel,
        grid=(steps,),
        in_specs=[src_spec, src_spec, src_ratio, src_ratio, chan_spec, chan_spec, chan_ratio, chan_ratio]
        + [table, pl.BlockSpec((MAXLAG, MAXLAG), lambda i: (0, 0))],
        out_specs=[out_spec] * outs,
        out_shape=[jax.ShapeDtypeStruct((rows // outs, LAGS), dtype) for dtype in dtypes],
        scratch_shapes=[
            pltpu.VMEM((rows, MAXLAG), jnp.float32),
            pltpu.VMEM((rows, MAXLAG), jnp.float32),
            pltpu.VMEM((2, sources, count, HALF), jnp.bfloat16),
            pltpu.VMEM((2, sources, count, HALF), jnp.bfloat16),
            pltpu.VMEM((2, STEP_K2, 2, sources, HALF), jnp.float32),
        ],
        compiler_params=pltpu.CompilerParams(vmem_limit_bytes=VMEM_LIMIT),
        cost_estimate=pl.CostEstimate(
            flops=4 * rows * SPAN * MAXLAG, bytes_accessed=8 * 1024 * 1024, transcendentals=0
        ),
        name="correlate",
    )(near, got, near, got, swap, got, swap, got, lags, tab["turn"])


def finish_kernel(own_ref, first_ref, second_ref, count_ref, out_ref):
    for at in range(0, LAGS, HALF):
        here = slice(at, at + HALF)
        total = own_ref[:, here] + first_ref[:, here].astype(jnp.float32)
        out_ref[:, here] = (total + second_ref[:, here].astype(jnp.float32)) / count_ref[...]


def finish(own, first, second, count):
    return pl.pallas_call(
        finish_kernel,
        out_shape=jax.ShapeDtypeStruct(own.shape, jnp.float32),
        compiler_params=pltpu.CompilerParams(vmem_limit_bytes=VMEM_LIMIT),
        name="finish",
    )(own, first, second, count)


def source_order(time_index, shape):
    row = lax.broadcasted_iota(jnp.int32, shape, 0)
    place = (row // 8) % 4
    parity = (time_index % 2 + row // 32) % 2
    near_by = jnp.where((place == 1) == (parity == 0), 1, 3)
    relative = jnp.where(place == 0, 2, jnp.where(place == 3, 0, near_by))
    z_hi = (time_index // 2 + relative) % 4
    return (2 * z_hi + parity) * 8 + row % 8


def body(record, fir_taps, sources, valid_mask):
    chan_count = lax.axis_size("chan")
    time_count = lax.axis_size("tm")
    _, channels, part_len = record.shape
    chan_local = channels // chan_count
    source_total = sources.shape[0]
    chan_index = lax.axis_index("chan")
    time_index = lax.axis_index("tm")
    first_chan = chan_index * chan_local

    sent = gather_rows(sources, record[0].T, chan_count)
    pieces = lax.all_to_all(sent, "chan", split_axis=0, concat_axis=0, tiled=True)

    tab = tables()
    products, rotations = in_vmem(tab["products"]), in_vmem(tab["rotations"])
    lags = in_vmem(tab["lags"])
    toeplitz = toeplitz_of(fir_taps, products, rotations)
    valid_float = valid_mask.astype(jnp.float32)
    every_source = jnp.arange(source_total, dtype=jnp.int32)
    every_channel = jnp.arange(channels, dtype=jnp.int32)
    order = source_order(time_index, (source_total, 1))
    ordered = jnp.sum(jnp.where(order == every_source[None, :], sources[None, :], 0), axis=1)
    own = first_chan + jnp.arange(chan_local, dtype=jnp.int32)
    rows = jnp.concatenate([ordered, own])
    window_valid = lax.dynamic_index_in_dim(valid_float, time_index, 0, keepdims=False)
    mask = jnp.sum(jnp.where(rows[:, None] == every_channel[None, :], window_valid[None, :], 0.0), axis=1)
    mask = jnp.broadcast_to(mask[:, None], (rows.shape[0], HALF))
    chan_valid = lax.dynamic_slice_in_dim(valid_float, first_chan, chan_local, 1)
    rows_out = source_total // time_count
    own_sources = lax.dynamic_slice_in_dim(sources, time_index * rows_out, rows_out, 0)
    own_picker = (own_sources[:, None] == every_channel[None, :]).astype(jnp.float32)
    own_valid = jnp.dot(own_picker, valid_float.T, precision=lax.Precision.HIGHEST)
    pair_count = jnp.dot(own_valid, chan_valid, precision=lax.Precision.HIGHEST)

    third = source_total // 2
    swap = front(pieces, toeplitz, products, rotations, mask, third, 2 * third, third)
    got = lax.ppermute(swap, "tm", [(j, j ^ 1) for j in range(time_count)])
    near = front(pieces, toeplitz, products, rotations, mask, 0, third, third)

    def along(way, values):
        steps = [2 * way * (1 - 2 * (j % 2)) for j in range(time_count)]
        return lax.ppermute(values, "tm", [(j, (j + steps[j]) % time_count) for j in range(time_count)])

    bf16, f32 = jnp.bfloat16, jnp.float32
    far, first = correlate(near, swap, got, lags, 0, (bf16, f32))
    far = along(1, far)
    second, own_part = correlate(near, swap, got, lags, 1, (bf16, f32))
    first = along(1, (first + far.astype(f32)).astype(bf16))
    second = along(-1, second)
    count = jnp.maximum(pair_count, 1.0)[:, :, None]
    count = jnp.broadcast_to(count, count.shape[:2] + (HALF,)).reshape(rows_out * chan_local, HALF)
    stack = finish(own_part, first, second, count)
    return stack.reshape(rows_out, chan_local, LAGS)


def solution(mesh):
    return jax.shard_map(
        body,
        mesh=mesh,
        in_specs=(P("tm", None, "chan"), P(), P(), P()),
        out_specs=P("tm", "chan", None),
        check_vma=False,
    )
```
